32 devices in a mesh: fsdp: 4 (over y, x), ctx: 4 (over z), tp: 2 (over core).
Axes of the slice: x: 2, y: 2, z: 4, core: 2. Of those that a mesh axis runs over, the one named last changes fastest.
Arguments:
- tokens: bfloat16 [4, 768, 2048], P('fsdp', 'ctx'), may hold values from -6 to 6
- out_grad: bfloat16 [4, 768, 2048], P('fsdp', 'ctx'), may hold values from -6 to 6
- lengths: int32 [4, 2], P('fsdp'), may hold values from 192 to 576, as said below
- w_query: bfloat16 [2048, 2048], P(('fsdp', 'ctx'), 'tp'), may hold values from -0.015625 to 0.015625
- w_key: bfloat16 [2048, 2048], P(('fsdp', 'ctx'), 'tp'), may hold values from -0.125 to 0.125
- w_value: bfloat16 [2048, 2048], P(('fsdp', 'ctx'), 'tp'), may hold values from -0.125 to 0.125
- w_out: bfloat16 [2048, 2048], P(('fsdp', 'ctx'), 'tp'), may hold values from -4 to 4
- w_gate: bfloat16 [2048, 5120], P(('fsdp', 'ctx'), 'tp'), may hold values from -0.125 to 0.125
- w_up: bfloat16 [2048, 5120], P(('fsdp', 'ctx'), 'tp'), may hold values from -0.125 to 0.125
- w_down: bfloat16 [2048, 5120], P(('fsdp', 'ctx'), 'tp'), may hold values from -0.125 to 0.125
- gain_attn: bfloat16 [2048], P(('fsdp', 'ctx')), may hold values from 0.5 to 1.5
- gain_ffn: bfloat16 [2048], P(('fsdp', 'ctx')), may hold values from 0.5 to 1.5
- bias_table: bfloat16 [32, 32], P('tp'), may hold values from -4 to 4
- clip_limit: float32 [32], P('tp'), may hold values from 0.5 to 6
Outputs:
- mixed_out: bfloat16 [4, 768, 2048], P('fsdp', 'ctx')
- grad_tokens: bfloat16 [4, 768, 2048], P('fsdp', 'ctx')
- grad_w_query: float32 [2048, 2048], P(('fsdp', 'ctx'), 'tp')
- grad_w_key: float32 [2048, 2048], P(('fsdp', 'ctx'), 'tp')
- grad_w_value: float32 [2048, 2048], P(('fsdp', 'ctx'), 'tp')
- grad_w_out: float32 [2048, 2048], P(('fsdp', 'ctx'), 'tp')
- grad_w_gate: float32 [2048, 5120], P(('fsdp', 'ctx'), 'tp')
- grad_w_up: float32 [2048, 5120], P(('fsdp', 'ctx'), 'tp')
- grad_w_down: float32 [2048, 5120], P(('fsdp', 'ctx'), 'tp')
- grad_gain_attn: float32 [2048], P(('fsdp', 'ctx'))
- grad_gain_ffn: float32 [2048], P(('fsdp', 'ctx'))
- grad_table: float32 [32, 32], P('tp')
- head_peaks: float32 [32], P('tp')
- clipped_query: bfloat16 [2048, 2048], P(('fsdp', 'ctx'), 'tp')
- clipped_key: bfloat16 [2048, 2048], P(('fsdp', 'ctx'), 'tp')
The draws below stay inside these ranges and needn't reach their ends.
Inputs may be any that keep to these rules, and one draw needn't show every extreme that they name: Each group holds two sequences packed from its first position, of lengths[g, 0] and lengths[g, 1], whose sum is at most 768; the rest is padding. Some group's first sequence has exactly 576.
All inputs are finite; a program needn't handle non-finite values.
Results may differ from the reference program's by a relative error of at most 0.024.
Values may be sent and summed in bfloat16 or wider, within the bound.
No kernel may reach another device: no remote copies, remote signals or barrier semaphores. Data moves between devices by JAX's collectives and lax.ppermute only.
A program may use at most 256 MiB of HBM per device.

```python
import math
import jax
import jax.numpy as jnp
from jax import lax

D = 2048
HEADS = 32
DK = 64
FF = 5120
BUCKETS = 32
HD = 2048
GROUPS = 4
SLOTS = 768
SHORTEST = 192
LONGEST = 576


def draw_lengths(key, part):
    first_key, second_key, third_key = jax.random.split(jax.random.fold_in(key, 17), 3)
    first = jax.random.randint(first_key, (GROUPS,), SHORTEST, LONGEST + 1)
    chosen = jax.random.randint(second_key, (), 0, GROUPS)
    first = jnp.where(jnp.arange(GROUPS) == chosen, LONGEST, first)
    room = jnp.minimum(SLOTS - first, LONGEST)
    spread = jax.random.randint(third_key, (GROUPS,), 0, LONGEST + 1)
    second = SHORTEST + spread % (room - SHORTEST + 1)
    return jnp.stack([first, second], axis=1).astype(jnp.int32)


def steps_of(rng, extent, cuts, least, top_value):
    level = 1.0
    for axis_at, parts in cuts:
        steps = jax.random.uniform(jax.random.fold_in(jax.random.fold_in(rng, 6), axis_at), (parts,), jnp.float32, least / len(cuts), top_value / len(cuts))
        level = level * jnp.repeat(jnp.exp(steps), extent[axis_at] // parts).reshape((-1,) + (1,) * (len(extent) - 1 - axis_at))
    return level


def scatter_about(rng, shape, deviation, most, cuts=(), kind=jnp.bfloat16):
    level = steps_of(rng, shape, cuts, -0.22, 0.18) if cuts else 1.0
    result = jax.random.normal(rng, shape, jnp.float32) * deviation * level
    return jnp.minimum(jnp.maximum(result, -most), most).astype(kind)


def setup_inputs(seed: int = 0) -> dict:
    arg_keys = jax.random.split(jax.random.key(seed), 15)
    tokens = scatter_about(arg_keys[0], (GROUPS, SLOTS, D), 1.0, 6.0, ((0, 4), (1, 4)))
    out_grad = scatter_about(arg_keys[1], (GROUPS, SLOTS, D), 1.0, 6.0, ((0, 4), (1, 4)))
    lengths = draw_lengths(jax.random.fold_in(arg_keys[14], 71), 0)
    w_query = scatter_about(arg_keys[3], (D, HD), (D * DK) ** -0.5, 0.015625, ((0, 16), (1, 2)))
    w_key = scatter_about(arg_keys[4], (D, HD), D ** -0.5, 0.125, ((0, 16), (1, 2)))
    w_value = scatter_about(arg_keys[5], (D, HD), D ** -0.5, 0.125, ((0, 16), (1, 2)))
    w_out = scatter_about(arg_keys[6], (D, HD), 2 ** -0.5, 4.0, ((0, 16), (1, 2)))
    w_gate = scatter_about(arg_keys[7], (D, FF), D ** -0.5, 0.125, ((0, 16), (1, 2)))
    w_up = scatter_about(arg_keys[8], (D, FF), D ** -0.5, 0.125, ((0, 16), (1, 2)))
    w_down = scatter_about(arg_keys[9], (D, FF), (FF // 2) ** -0.5, 0.125, ((0, 16), (1, 2)))
    gain_attn = jnp.clip(1.0 + 0.1 * jax.random.normal(arg_keys[10], (D,), jnp.float32), 0.5, 1.5).astype(jnp.bfloat16)
    gain_ffn = jnp.clip(1.0 + 0.1 * jax.random.normal(arg_keys[11], (D,), jnp.float32), 0.5, 1.5).astype(jnp.bfloat16)
    bias_table = scatter_about(arg_keys[12], (HEADS, BUCKETS), 1.0, 4.0, ((0, 2),))
    clip_limit = jnp.clip(jnp.exp(math.log(6.0) - 2.4849066 * jax.random.uniform(arg_keys[13], (HEADS,), jnp.float32) ** steps_of(arg_keys[13], (HEADS,), ((0, 2),), -0.2, 0.2)), 0.5, 6.0)
    return dict(tokens=tokens, out_grad=out_grad, lengths=lengths, w_query=w_query, w_key=w_key, w_value=w_value, w_out=w_out, w_gate=w_gate, w_up=w_up, w_down=w_down, gain_attn=gain_attn, gain_ffn=gain_ffn, bias_table=bias_table, clip_limit=clip_limit)


@jax.custom_vjp
def low(v):
    return lax.optimization_barrier(v.astype(jnp.bfloat16)).astype(jnp.float32)

@jax.custom_vjp
def low_back(v):
    return v

def low_keep(v):
    return (low(v), None)

def low_pass(kept, grad):
    return (grad,)

def back_keep(v):
    return (v, None)

def back_low(kept, grad):
    return (low(grad),)
low.defvjp(low_keep, low_pass)
low_back.defvjp(back_keep, back_low)
THRESHOLDS = (12, 16, 23, 32, 46, 64, 91)
NEGATIVE = -1e+30
EPSILON = 1e-06

def bucket_of(offset):
    distance = jnp.abs(offset).astype(jnp.int32)
    beyond = 8 + sum(((distance >= threshold).astype(jnp.int32) for threshold in THRESHOLDS))
    within = jnp.where(distance < 8, distance, beyond)
    return (within + jnp.where(offset > 0, BUCKETS // 2, 0)).astype(jnp.int32)

def segment_of(place, length_pair):
    first_end = length_pair[0]
    second_end = length_pair[0] + length_pair[1]
    return ((place >= first_end).astype(jnp.int32) + (place >= second_end).astype(jnp.int32)).astype(jnp.int32)

def normalize(values, gain_row):
    return values * lax.rsqrt(lax.optimization_barrier(jnp.mean(values * values, axis=-1, keepdims=True)) + EPSILON) * gain_row

def matmul(left_side, right_side):
    return jnp.dot(left_side, right_side, precision=lax.Precision.HIGHEST)

def attend(queries, key_rows, value_rows, table_in, length_pair):
    slot_count = key_rows.shape[0]
    query_block = math.gcd(slot_count, 512)
    key_heads = key_rows.reshape(slot_count, HEADS, DK)
    value_heads = value_rows.reshape(slot_count, HEADS, DK)
    key_place = jnp.arange(slot_count, dtype=jnp.int32)
    key_segment = segment_of(key_place, length_pair)
    starts = jnp.arange(0, slot_count, query_block, dtype=jnp.int32)
    blocks = queries.reshape(slot_count // query_block, query_block, HEADS, DK)

    def one_block(block_pair):
        query_heads, first_row = block_pair
        query_place = first_row + jnp.arange(query_block, dtype=jnp.int32)
        query_segment = segment_of(query_place, length_pair)
        logits = low_back(jnp.einsum('qhd,khd->hqk', query_heads, key_heads, precision=lax.Precision.HIGHEST))
        offsets = bucket_of(key_place[None, :] - query_place[:, None])
        same_part = query_segment[:, None] == key_segment[None, :]
        scores = jnp.where(same_part[None], logits + table_in[:, offsets], NEGATIVE)
        log_total = jax.nn.logsumexp(scores, axis=2, keepdims=True)
        chance = low(jnp.exp(scores - log_total))
        mixed_rows = jnp.einsum('hqk,khd->qhd', chance, value_heads, precision=lax.Precision.HIGHEST)
        both_valid = same_part & (query_segment < 2)[:, None]
        head_peak = lax.optimization_barrier(jnp.max(jnp.where(both_valid[None], logits, NEGATIVE), axis=(1, 2)))
        return (mixed_rows.reshape(query_block, HEADS * DK), head_peak)
    mixed_rows, head_peak = lax.map(jax.checkpoint(one_block), (blocks, starts))
    return (mixed_rows.reshape(slot_count, HEADS * DK), lax.optimization_barrier(jnp.max(head_peak, axis=0)))

def layer_forward(inputs, lengths, w_query, w_key, w_value, w_out, w_gate, w_up, w_down, gain_attn, gain_ffn, table_in):

    def one_group(group_pair):
        rows_in, length_pair = group_pair
        normed = low(normalize(rows_in, gain_attn))
        queries = low_back(low(matmul(normed, w_query)))
        key_rows = low_back(low(matmul(normed, w_key)))
        value_rows = low_back(low(matmul(normed, w_value)))
        mixed_rows, head_peak = attend(queries, key_rows, value_rows, table_in, length_pair)
        mixed_rows = low_back(low(mixed_rows))
        branch = low_back(matmul(mixed_rows, w_out.T))
        hidden_state = rows_in + branch
        normed_ffn = low(normalize(hidden_state, gain_ffn))
        gate_pre = low_back(matmul(normed_ffn, w_gate))
        upward = low_back(matmul(normed_ffn, w_up))
        product = low(jax.nn.gelu(gate_pre, approximate=True) * upward)
        return (hidden_state + low_back(matmul(product, w_down.T)), head_peak)
    outputs, head_peak = lax.map(jax.checkpoint(one_group), (inputs, lengths))
    return (outputs, lax.optimization_barrier(jnp.max(head_peak, axis=0)))

def reference(tokens, out_grad, lengths, w_query, w_key, w_value, w_out, w_gate, w_up, w_down, gain_attn, gain_ffn, bias_table, clip_limit):
    inputs = tokens.astype(jnp.float32)
    params = tuple((weight.astype(jnp.float32) for weight in (w_query, w_key, w_value, w_out, w_gate, w_up, w_down, gain_attn, gain_ffn, bias_table)))

    def forward(rows_all, *weights):
        return layer_forward(rows_all, lengths, *weights)
    outputs, pullback, head_peaks = jax.vjp(forward, inputs, *params, has_aux=True)
    totals = (lengths[:, 0] + lengths[:, 1]).astype(jnp.int32)
    valid_rows = (jnp.arange(SLOTS, dtype=jnp.int32)[None, :] < totals[:, None]).astype(jnp.float32)
    gradients = pullback(out_grad.astype(jnp.float32) * valid_rows[:, :, None])
    factor = jnp.sqrt(clip_limit / jnp.maximum(head_peaks, clip_limit))

    def clipped(weight):
        scaled = weight.astype(jnp.float32).reshape(D, HEADS, DK) * factor[None, :, None]
        return scaled.reshape(D, HEADS * DK).astype(jnp.bfloat16)
    return (outputs.astype(jnp.bfloat16), gradients[0].astype(jnp.bfloat16), gradients[1], gradients[2], gradients[3], gradients[4], gradients[5], gradients[6], gradients[7], gradients[8], gradients[9], gradients[10], head_peaks, clipped(w_query), clipped(w_key))
```

```python
import functools

import jax
import jax.numpy as jnp
from jax import lax
from jax.experimental import pallas as pl
from jax.experimental.pallas import tpu as pltpu
from jax.sharding import PartitionSpec as P

DK = 64
BUCKETS = 32
THRESHOLDS = (12, 16, 23, 32, 46, 64, 91)
NEGATIVE = -1e30
EPSILON = 1e-06
QUERY_BLOCK = 256
NEAR = 512
VMEM_LIMIT = 48 * 1024 * 1024
LOW = jnp.bfloat16
WIDE = jnp.float32


def bucket_of(offset):
    distance = jnp.abs(offset)
    beyond = 8 + sum(((distance >= threshold).astype(jnp.int32) for threshold in THRESHOLDS))
    within = jnp.where(distance < 8, distance, beyond)
    return within + jnp.where(offset > 0, BUCKETS // 2, 0)


def contract(left, right, left_dim, right_dim):
    return lax.dot_general(
        left, right, (((left_dim,), (right_dim,)), ((), ())), preferred_element_type=WIDE
    )


def places(meta_ref, count, half):
    here, core = meta_ref[0], meta_ref[1]
    for side in range(2):
        for back in range(count):
            block = lax.rem(here - back + count, count) * 2 + (core if side == 0 else 1 - core)
            yield (side * count + back) * half, pl.multiple_of(block * half, half)


def segments_down(meta_ref, shape):
    place = lax.broadcasted_iota(jnp.int32, shape, 0)
    return (place >= meta_ref[2]).astype(jnp.int32) + (place >= meta_ref[3]).astype(jnp.int32)


def segments_across(meta_ref, first, width):
    place = first + lax.broadcasted_iota(jnp.int32, (1, width), 1)
    return (place >= meta_ref[2]).astype(jnp.int32) + (place >= meta_ref[3]).astype(jnp.int32)


def forward_kernel(
    meta_ref, rows_ref, bias_ref, mixed_ref, log_ref, peak_ref, home_ref, flip_ref, part_ref, *, count, half, heads
):
    slots, width, block = 2 * count * half, heads * DK, QUERY_BLOCK
    for source, target in places(meta_ref, count, half):
        home_ref[pl.ds(target, half), :] = rows_ref[source : source + half, :]
    part_ref[...] = segments_down(meta_ref, (slots, block))
    log_ref[...] = jnp.zeros_like(log_ref)
    peak_ref[...] = jnp.full(peak_ref.shape, NEGATIVE, WIDE)
    for head in range(heads):
        at = head * DK
        keys = home_ref[:, width + at : width + at + DK]
        queries_flip = home_ref[:, at : at + DK].T
        values_flip = home_ref[:, 2 * width + at : 2 * width + at + DK].T
        peak = jnp.full((1, block), NEGATIVE, WIDE)
        for step in range(slots // block):
            first = step * block
            across = segments_across(meta_ref, first, block)
            logits = contract(keys, queries_flip[:, first : first + block], 1, 0)
            logits = jnp.where(part_ref[...] == across, logits, NEGATIVE)
            tops = jnp.max(logits, axis=0, keepdims=True)
            peak = jnp.maximum(peak, jnp.where(across < 2, tops, NEGATIVE))
            start = slots - block - first
            scores = logits + bias_ref[head, start : start + slots, :]
            highest = jnp.max(scores, axis=0, keepdims=True)
            weights = jnp.exp(scores - highest)
            total = jnp.sum(weights, axis=0, keepdims=True)
            mixed = contract(values_flip, weights.astype(LOW), 1, 0)
            flip_ref[at : at + DK, first : first + block] = mixed / total
            log_ref[head : head + 1, first : first + block] = highest + jnp.log(total)
        peak_ref[head : head + 1, :] = jnp.broadcast_to(
            jnp.max(peak, axis=1, keepdims=True), (1, peak_ref.shape[1])
        )
    home_ref[:, :width] = flip_ref[...].T.astype(LOW)
    for source, target in places(meta_ref, count, half):
        mixed_ref[source : source + half, :] = home_ref[pl.ds(target, half), :width]


def backward_kernel(
    meta_ref,
    rows_ref,
    grad_ref,
    log_ref,
    bias_ref,
    out_ref,
    table_ref,
    home_ref,
    grad_home_ref,
    flip_ref,
    part_ref,
    sums_ref,
    down_ref,
    *,
    count,
    half,
    heads,
):
    slots, width, block = 2 * count * half, heads * DK, QUERY_BLOCK
    for source, target in places(meta_ref, count, half):
        home_ref[pl.ds(target, half), :] = rows_ref[source : source + half, :]
        grad_home_ref[pl.ds(target, half), :] = grad_ref[source : source + half, :]
    part_ref[...] = segments_down(meta_ref, (slots, block))
    table_ref[...] = jnp.zeros_like(table_ref)
    lane = lax.broadcasted_iota(jnp.int32, (1, table_ref.shape[1]), 1)
    near = slots - block - (NEAR - block) // 2
    buckets = bucket_of(
        lax.broadcasted_iota(jnp.int32, (NEAR, block), 0)
        + near
        - (slots - block)
        - lax.broadcasted_iota(jnp.int32, (NEAR, block), 1)
    )
    for head in range(heads):
        at = head * DK
        queries = home_ref[:, at : at + DK]
        keys = home_ref[:, width + at : width + at + DK]
        values = home_ref[:, 2 * width + at : 2 * width + at + DK]
        grads = grad_home_ref[:, at : at + DK]
        queries_flip, keys_flip, grads_flip = queries.T, keys.T, grads.T
        sums_ref[...] = jnp.zeros_like(sums_ref)
        for step in range(slots // block):
            first = step * block
            across = segments_across(meta_ref, first, block)
            start = slots - block - first
            logits = contract(keys, queries_flip[:, first : first + block], 1, 0)
            scores = logits + bias_ref[head, start : start + slots, :]
            scores = scores - log_ref[head : head + 1, first : first + block]
            chance = jnp.exp(jnp.where(part_ref[...] == across, scores, NEGATIVE))
            grad_chance = contract(values, grads_flip[:, first : first + block], 1, 0)
            delta = jnp.sum(chance * grad_chance, axis=0, keepdims=True)
            grad_scores = chance * (grad_chance - delta)
            sums_ref[start : start + slots, :] += grad_scores
            rounded = grad_scores.astype(LOW)
            grad_keys = contract(rounded, queries[first : first + block, :], 1, 0)
            grad_values = contract(chance.astype(LOW), grads[first : first + block, :], 1, 0)
            if step == 0:
                down_ref[:, :DK] = grad_keys
                down_ref[:, DK:] = grad_values
            else:
                down_ref[:, :DK] += grad_keys
                down_ref[:, DK:] += grad_values
            flip_ref[at : at + DK, first : first + block] = contract(keys_flip, rounded, 1, 0)
        home_ref[:, width + at : width + at + DK] = down_ref[:, :DK].astype(LOW)
        home_ref[:, 2 * width + at : 2 * width + at + DK] = down_ref[:, DK:].astype(LOW)
        close = sums_ref[near : near + NEAR, :]
        row = jnp.where(lane == BUCKETS // 2 - 1, jnp.sum(sums_ref[:near, :]), 0.0)
        row = row + jnp.where(lane == BUCKETS - 1, jnp.sum(sums_ref[near + NEAR :, :]), 0.0)
        for bucket in range(BUCKETS):
            row = row + jnp.where(lane == bucket, jnp.sum(jnp.where(buckets == bucket, close, 0.0)), 0.0)
        table_ref[head : head + 1, :] = row
    home_ref[:, :width] = flip_ref[...].T.astype(LOW)
    for source, target in places(meta_ref, count, half):
        out_ref[source : source + half, :] = home_ref[pl.ds(target, half), :]


def bias_master(table, slots):
    heads, block = table.shape[0], QUERY_BLOCK
    near = slots - block - (NEAR - block) // 2
    offset = (
        lax.broadcasted_iota(jnp.int32, (NEAR, block), 0)
        + near
        - (slots - block)
        - lax.broadcasted_iota(jnp.int32, (NEAR, block), 1)
    )
    buckets = bucket_of(offset)[None]
    close = jnp.zeros((heads, NEAR, block), WIDE)
    for bucket in range(BUCKETS):
        close = jnp.where(buckets == bucket, table[:, bucket][:, None, None], close)
    after = 2 * slots - block - near - NEAR
    below = jnp.broadcast_to(table[:, BUCKETS // 2 - 1][:, None, None], (heads, near, block))
    above = jnp.broadcast_to(table[:, BUCKETS - 1][:, None, None], (heads, after, block))
    return jnp.concatenate([below, close, above], axis=1)


def whole(memory=pltpu.VMEM):
    return pl.BlockSpec(memory_space=memory)


def attend_forward(meta, rows_in, bias, count, half, heads):
    slots, width, block = 2 * count * half, heads * DK, QUERY_BLOCK
    return pl.pallas_call(
        functools.partial(forward_kernel, count=count, half=half, heads=heads),
        out_shape=(
            jax.ShapeDtypeStruct((slots, width), LOW),
            jax.ShapeDtypeStruct((8, slots), WIDE),
            jax.ShapeDtypeStruct((8, 128), WIDE),
        ),
        in_specs=[whole(pltpu.SMEM), whole(), whole()],
        out_specs=(whole(), whole(), whole()),
        scratch_shapes=[
            pltpu.VMEM((slots, 3 * width), LOW),
            pltpu.VMEM((width, slots), WIDE),
            pltpu.VMEM((slots, block), jnp.int32),
        ],
        compiler_params=pltpu.CompilerParams(vmem_limit_bytes=VMEM_LIMIT),
        cost_estimate=pl.CostEstimate(
            flops=4 * heads * slots * slots * DK,
            bytes_accessed=8 * slots * width + 8 * heads * slots * block,
            transcendentals=heads * slots * slots,
        ),
        name="attend_forward",
    )(meta, rows_in, bias)


def attend_backward(meta, rows_in, grad_in, log_total, bias, count, half, heads):
    slots, width, block = 2 * count * half, heads * DK, QUERY_BLOCK
    return pl.pallas_call(
        functools.partial(backward_kernel, count=count, half=half, heads=heads),
        out_shape=(
            jax.ShapeDtypeStruct((slots, 3 * width), LOW),
            jax.ShapeDtypeStruct((8, 128), WIDE),
        ),
        in_specs=[whole(pltpu.SMEM), whole(), whole(), whole(), whole()],
        out_specs=(whole(), whole()),
        scratch_shapes=[
            pltpu.VMEM((slots, 3 * width), LOW),
            pltpu.VMEM((slots, width), LOW),
            pltpu.VMEM((width, slots), WIDE),
            pltpu.VMEM((slots, block), jnp.int32),
            pltpu.VMEM((2 * slots - block, block), WIDE),
            pltpu.VMEM((slots, 2 * DK), WIDE),
        ],
        compiler_params=pltpu.CompilerParams(vmem_limit_bytes=VMEM_LIMIT),
        cost_estimate=pl.CostEstimate(
            flops=10 * heads * slots * slots * DK,
            bytes_accessed=16 * slots * width + 8 * heads * slots * block,
            transcendentals=heads * slots * slots,
        ),
        name="attend_backward",
    )(meta, rows_in, grad_in, log_total, bias)


def shards(
    tokens,
    out_grad,
    lengths,
    w_query,
    w_key,
    w_value,
    w_out,
    w_gate,
    w_up,
    w_down,
    gain_attn,
    gain_ffn,
    bias_table,
    clip_limit,
):
    groups, count, cores = (lax.axis_size(name) for name in ("fsdp", "ctx", "tp"))
    assert cores == 2
    group, here, core = (lax.axis_index(name) for name in ("fsdp", "ctx", "tp"))
    half = tokens.shape[1] // cores
    slots = tokens.shape[1] * count
    heads = bias_table.shape[0] // count
    head_width = heads * DK
    unit_width = w_gate.shape[1] // count
    weight_rows = w_query.shape[0]

    def around(value, steps):
        return lax.ppermute(value, "ctx", [(i, (i + steps) % count) for i in range(count)])

    def flip(value, mask):
        return lax.ppermute(value, "fsdp", [(i, i ^ mask) for i in range(groups)])

    def swap(value):
        return lax.ppermute(value, "tp", [(0, 1), (1, 0)])

    def ordered(pieces, which, axis):
        total = len(pieces)
        if total > 4:
            stacked = jnp.stack(pieces)
            return jnp.concatenate(
                [lax.dynamic_index_in_dim(stacked, which(n), 0, False) for n in range(total)], axis=axis
            )
        return jnp.concatenate([lax.select_n(which(n), *pieces) for n in range(total)], axis=axis)

    def place_of(n):
        return lax.rem(here - n + count, count)

    def spread(parts, width):
        def block(steps):
            start = lax.rem(here + steps, count) * width
            return jnp.concatenate([lax.dynamic_slice_in_dim(p, start, width, 1) for p in parts], axis=1)

        pieces = [block(0)] + [around(block(k), k) for k in range(1, count)]
        return ordered(pieces, place_of, 0)

    def collect(block, width):
        def rows_of(steps):
            start = lax.rem(here + steps, count) * weight_rows
            return lax.dynamic_slice_in_dim(block, start, weight_rows, 0)

        pieces = [rows_of(0)] + [around(rows_of(k), k) for k in range(1, count)]
        return [
            ordered([p[:, at : at + width] for p in pieces], place_of, 1).astype(WIDE)
            for at in range(0, block.shape[1], width)
        ]

    def gather_weights(block):
        if groups != 4:
            return lax.all_gather(block, "fsdp", axis=0, tiled=True)
        middle = block.shape[0] // 2
        first, second = flip(block, 1), flip(block, 2)
        corner = jnp.concatenate([flip(first[:middle], 2), flip(second[middle:], 1)], axis=0)
        return ordered([block, first, second, corner], lambda n: group ^ n, 0)

    def gather_rows(piece):
        mine = jnp.concatenate([piece] + [around(piece, k) for k in range(1, count)], axis=0)
        return jnp.concatenate([mine, swap(mine)], axis=0)

    def reduce_rows(product_of):
        own = count * half
        theirs = swap(product_of(own, 2 * own).astype(LOW))
        total = product_of(0, own) + theirs.astype(WIDE)
        low = total.astype(LOW)
        result = total[:half]
        for k in range(1, count):
            result = result + around(low[k * half : (k + 1) * half], -k).astype(WIDE)
        return result

    def both_cores(piece):
        other = swap(piece)
        return jnp.where(
            core == 0, jnp.concatenate([piece, other], axis=0), jnp.concatenate([other, piece], axis=0)
        )

    def own_rows(value):
        return lax.dynamic_slice_in_dim(value[0], core * half, half, 0)

    def inverse_norm(value):
        return lax.rsqrt(jnp.mean(value * value, axis=-1, keepdims=True) + EPSILON)

    def norm_back(value, inverse, grad):
        along = jnp.mean(grad * value, axis=-1, keepdims=True)
        return inverse * grad - value * (inverse * inverse * inverse * along)

    ends = (lengths[0, 0], lengths[0, 0] + lengths[0, 1])
    meta = jnp.stack([here, core, ends[0], ends[1]]).astype(jnp.int32)
    attn_gain = gain_attn.astype(WIDE)[:, None]
    ffn_gain = gain_ffn.astype(WIDE)[:, None]

    def scaled(weight, gain):
        return (weight.astype(WIDE) * gain).astype(LOW)

    query_key_value = [scaled(w, attn_gain) for w in (w_query, w_key, w_value)]
    gate_up = [scaled(w, ffn_gain) for w in (w_gate, w_up)]

    attn_columns = gather_weights(spread(query_key_value, head_width))
    inputs = own_rows(tokens).astype(WIDE)
    inverse_one = inverse_norm(inputs)
    normed = gather_rows((inputs * inverse_one).astype(LOW))
    out_columns = gather_weights(spread([w_out], head_width))
    gate_up_columns = lax.all_gather(spread(gate_up, unit_width), "fsdp", axis=0, tiled=True)
    down_columns = lax.all_gather(spread([w_down], unit_width), "fsdp", axis=0, tiled=True)

    row_place = (here * cores + core) * half + jnp.arange(half, dtype=jnp.int32)
    row_valid = (row_place < ends[1])[:, None]
    grad_out = jnp.where(row_valid, own_rows(out_grad).astype(WIDE), 0.0)
    grad_rows = gather_rows(grad_out.astype(LOW))

    my_table = lax.dynamic_slice_in_dim(bias_table, here * heads, heads, 0).astype(WIDE)
    bias = bias_master(my_table, slots)

    projected = contract(normed, attn_columns, 1, 0).astype(LOW)
    mixed, log_total, peaks = attend_forward(meta, projected, bias, count, half, heads)
    hidden = inputs + reduce_rows(lambda a, b: contract(mixed[a:b], out_columns, 1, 1))
    inverse_two = inverse_norm(hidden)
    normed_ffn = gather_rows((hidden * inverse_two).astype(LOW))
    both_pre = contract(normed_ffn, gate_up_columns, 1, 0)
    gate_pre, upward = both_pre[:, :unit_width], both_pre[:, unit_width:]
    activated, gelu_back = jax.vjp(functools.partial(jax.nn.gelu, approximate=True), gate_pre)
    product = (activated * upward).astype(LOW)
    ffn_out = reduce_rows(lambda a, b: contract(product[a:b], down_columns, 1, 1))
    mixed_out = both_cores((hidden + ffn_out).astype(LOW))[None]

    grad_product = contract(grad_rows, down_columns, 1, 0)
    grad_gate = gelu_back(grad_product * upward)[0].astype(LOW)
    grad_upward = (grad_product * activated).astype(LOW)
    grad_both = jnp.concatenate([grad_gate, grad_upward], axis=1)
    grad_normed_ffn = reduce_rows(lambda a, b: contract(grad_both[a:b], gate_up_columns, 1, 1))
    grad_hidden = grad_out + norm_back(hidden, inverse_two, grad_normed_ffn)
    branch_rows = gather_rows(grad_hidden.astype(LOW))

    def sum_groups(left, right):
        terms = contract(left, right, 0, 0).astype(LOW)
        return lax.psum_scatter(terms, "fsdp", scatter_dimension=0, tiled=True)

    (grad_down,) = collect(sum_groups(grad_rows, product), unit_width)
    grad_gate_w, grad_up_w = collect(sum_groups(normed_ffn, grad_both), unit_width)

    grad_mixed = contract(branch_rows, out_columns, 1, 0).astype(LOW)
    grad_projected, table_terms = attend_backward(
        meta, projected, grad_mixed, log_total, bias, count, half, heads
    )
    (grad_out_w,) = collect(sum_groups(branch_rows, mixed), head_width)
    grad_normed = reduce_rows(lambda a, b: contract(grad_projected[a:b], attn_columns, 1, 1))
    grad_tokens = both_cores((grad_hidden + norm_back(inputs, inverse_one, grad_normed)).astype(LOW))[None]
    grad_query_w, grad_key_w, grad_value_w = collect(sum_groups(normed, grad_projected), head_width)

    def gain_terms(weights, grads):
        return sum(jnp.sum(w.astype(WIDE) * g, axis=1) for w, g in zip(weights, grads, strict=True))

    gain_grads = jnp.stack(
        [
            gain_terms((w_query, w_key, w_value), (grad_query_w, grad_key_w, grad_value_w)),
            gain_terms((w_gate, w_up), (grad_gate_w, grad_up_w)),
        ]
    )
    gain_grads = gain_grads + swap(gain_grads)

    small = jnp.concatenate([table_terms[:heads, :BUCKETS], peaks[:heads, :1]], axis=1)
    blank = jnp.concatenate([jnp.zeros((1, BUCKETS), WIDE), jnp.full((1, 1), NEGATIVE, WIDE)], axis=1)
    is_sum = jnp.arange(BUCKETS + 1)[None, :] < BUCKETS
    small = jnp.where(
        (jnp.arange(count * heads) // heads == here)[:, None],
        jnp.tile(small, (count, 1)),
        blank,
    )

    def merge(first, second):
        return jnp.where(is_sum, first + second, jnp.maximum(first, second))

    mask = 1
    while mask < groups:
        small = merge(small, flip(small, mask))
        mask *= 2
    mask = 1
    while mask < count:
        small = merge(small, lax.ppermute(small, "ctx", [(i, i ^ mask) for i in range(count)]))
        mask *= 2
    grad_table, head_peaks = small[:, :BUCKETS], small[:, BUCKETS]
    factor = jnp.sqrt(clip_limit / jnp.maximum(head_peaks, clip_limit))
    factor_row = jnp.repeat(factor, DK)[None, :]

    def clipped(weight):
        return (weight.astype(WIDE) * factor_row).astype(LOW)

    return (
        mixed_out,
        grad_tokens,
        grad_query_w * attn_gain,
        grad_key_w * attn_gain,
        grad_value_w * attn_gain,
        grad_out_w,
        grad_gate_w * ffn_gain,
        grad_up_w * ffn_gain,
        grad_down,
        gain_grads[0],
        gain_grads[1],
        grad_table,
        head_peaks,
        clipped(w_query),
        clipped(w_key),
    )


def solution(mesh):
    rows, weight, gain = P("fsdp", "ctx", None), P(("fsdp", "ctx"), "tp"), P(("fsdp", "ctx"))
    return jax.shard_map(
        shards,
        mesh=mesh,
        in_specs=(rows, rows, P("fsdp", None)) + (weight,) * 7 + (gain, gain, P("tp", None), P("tp")),
        out_specs=(rows, rows) + (weight,) * 7 + (gain, gain, P("tp", None), P("tp"), weight, weight),
        check_vma=False,
    )
```

```python
import functools
import math

import jax
import jax.numpy as jnp
from jax import lax
from jax.experimental import pallas as pl
from jax.experimental.pallas import tpu as pltpu
from jax.sharding import PartitionSpec as P

DK = 64
BUCKETS = 32
THRESHOLDS = (12, 16, 23, 32, 46, 64, 91)
NEGATIVE = -1e30
EPSILON = 1e-06
QUERY_BLOCK = 256
TILE = 128
VMEM_LIMIT = 48 * 1024 * 1024
LOW = jnp.bfloat16
WIDE = jnp.float32


def lasting(micros):
    return pl.CostEstimate(flops=int(micros * 1.1e9), bytes_accessed=int(micros * 3.3e6), transcendentals=0)


def bucket_of(offset):
    distance = jnp.abs(offset)
    beyond = 8 + sum(((distance >= threshold).astype(jnp.int32) for threshold in THRESHOLDS))
    within = jnp.where(distance < 8, distance, beyond)
    return within + jnp.where(offset > 0, BUCKETS // 2, 0)


def contract(left, right, left_dim, right_dim):
    return lax.dot_general(
        left, right, (((left_dim,), (right_dim,)), ((), ())), preferred_element_type=WIDE
    )


def segments_down(meta_ref, shape):
    place = lax.broadcasted_iota(jnp.int32, shape, 0)
    return (place >= meta_ref[0]).astype(jnp.int32) + (place >= meta_ref[1]).astype(jnp.int32)


def segments_across(meta_ref, first, width):
    place = first + lax.broadcasted_iota(jnp.int32, (1, width), 1)
    return (place >= meta_ref[0]).astype(jnp.int32) + (place >= meta_ref[1]).astype(jnp.int32)


def forward_kernel(
    meta_ref, rows_ref, bias_ref, mixed_ref, log_ref, peak_ref, flip_ref, part_ref, *, slots, heads
):
    width, block = heads * DK, QUERY_BLOCK
    part_ref[...] = segments_down(meta_ref, (slots, block))
    log_ref[...] = jnp.zeros_like(log_ref)
    peak_ref[...] = jnp.full(peak_ref.shape, NEGATIVE, WIDE)
    for head in range(heads):
        at = head * DK
        keys = rows_ref[:, width + at : width + at + DK]
        queries_flip = rows_ref[:, at : at + DK].T
        values_flip = rows_ref[:, 2 * width + at : 2 * width + at + DK].T
        peak = jnp.full((1, block), NEGATIVE, WIDE)
        for step in range(slots // block):
            first = step * block
            across = segments_across(meta_ref, first, block)
            logits = contract(keys, queries_flip[:, first : first + block], 1, 0)
            logits = jnp.where(part_ref[...] == across, logits, NEGATIVE)
            tops = jnp.max(logits, axis=0, keepdims=True)
            peak = jnp.maximum(peak, jnp.where(across < 2, tops, NEGATIVE))
            start = slots - block - first
            scores = logits + bias_ref[head, start : start + slots, :]
            highest = jnp.max(scores, axis=0, keepdims=True)
            weights = jnp.exp(scores - highest)
            total = jnp.sum(weights, axis=0, keepdims=True)
            mixed = contract(values_flip, weights.astype(LOW), 1, 0)
            flip_ref[at : at + DK, first : first + block] = mixed / total
            log_ref[head : head + 1, first : first + block] = highest + jnp.log(total)
        peak_ref[head : head + 1, :] = jnp.broadcast_to(
            jnp.max(peak, axis=1, keepdims=True), (1, peak_ref.shape[1])
        )
    mixed_ref[...] = flip_ref[...].T.astype(LOW)


def backward_kernel(
    meta_ref,
    rows_ref,
    grad_ref,
    log_ref,
    bias_ref,
    out_ref,
    table_ref,
    flip_ref,
    part_ref,
    sums_ref,
    down_ref,
    *,
    slots,
    heads,
):
    width, block = heads * DK, QUERY_BLOCK
    part_ref[...] = segments_down(meta_ref, (slots, block))
    table_ref[...] = jnp.zeros_like(table_ref)
    lane = lax.broadcasted_iota(jnp.int32, (1, table_ref.shape[1]), 1)
    offsets = tile_offsets()
    marks = [bucket_of(offsets + shift * TILE) for shift in (-1, 0, 1)]
    for head in range(heads):
        at = head * DK
        queries = rows_ref[:, at : at + DK]
        keys = rows_ref[:, width + at : width + at + DK]
        values = rows_ref[:, 2 * width + at : 2 * width + at + DK]
        grads = grad_ref[:, at : at + DK]
        queries_flip, keys_flip, grads_flip = queries.T, keys.T, grads.T
        sums_ref[...] = jnp.zeros_like(sums_ref)
        for step in range(slots // block):
            first = step * block
            across = segments_across(meta_ref, first, block)
            start = slots - block - first
            logits = contract(keys, queries_flip[:, first : first + block], 1, 0)
            scores = logits + bias_ref[head, start : start + slots, :]
            scores = scores - log_ref[head : head + 1, first : first + block]
            chance = jnp.exp(jnp.where(part_ref[...] == across, scores, NEGATIVE))
            grad_chance = contract(values, grads_flip[:, first : first + block], 1, 0)
            delta = jnp.sum(chance * grad_chance, axis=0, keepdims=True)
            grad_scores = chance * (grad_chance - delta)
            sums_ref[start : start + slots, :] += grad_scores
            rounded = grad_scores.astype(LOW)
            grad_keys = contract(rounded, queries[first : first + block, :], 1, 0)
            grad_values = contract(chance.astype(LOW), grads[first : first + block, :], 1, 0)
            if step == 0:
                down_ref[:, :DK] = grad_keys
                down_ref[:, DK:] = grad_values
            else:
                down_ref[:, :DK] += grad_keys
                down_ref[:, DK:] += grad_values
            flip_ref[at : at + DK, first : first + block] = contract(keys_flip, rounded, 1, 0)
        out_ref[:, width + at : width + at + DK] = down_ref[:, :DK].astype(LOW)
        out_ref[:, 2 * width + at : 2 * width + at + DK] = down_ref[:, DK:].astype(LOW)
        near = [jnp.zeros((TILE, TILE), WIDE) for _ in marks]
        far = [jnp.zeros((TILE, TILE), WIDE) for _ in range(2)]
        for down in range((2 * slots - block) // TILE):
            for across in range(block // TILE):
                shift = down - (slots - block) // TILE - across
                tile = sums_ref[down * TILE : (down + 1) * TILE, across * TILE : (across + 1) * TILE]
                if abs(shift) < 2:
                    near[shift + 1] = near[shift + 1] + tile
                else:
                    far[int(shift > 0)] = far[int(shift > 0)] + tile
        row = jnp.where(lane == BUCKETS // 2 - 1, jnp.sum(far[0]), 0.0)
        row = row + jnp.where(lane == BUCKETS - 1, jnp.sum(far[1]), 0.0)
        for bucket in range(BUCKETS):
            held = sum(
                jnp.where(mark == bucket, tile, 0.0) for mark, tile in zip(marks, near, strict=True)
            )
            row = row + jnp.where(lane == bucket, jnp.sum(held), 0.0)
        table_ref[head : head + 1, :] = row
    out_ref[:, :width] = flip_ref[...].T.astype(LOW)


def tile_offsets():
    return lax.broadcasted_iota(jnp.int32, (TILE, TILE), 0) - lax.broadcasted_iota(jnp.int32, (TILE, TILE), 1)


def bias_kernel(table_ref, out_ref, *, slots, heads):
    block = QUERY_BLOCK
    offsets = tile_offsets()
    buckets = [bucket_of(offsets + shift * TILE) for shift in (-1, 0, 1)]
    for head in range(heads):
        tiles = []
        for marks in buckets:
            tile = jnp.full((TILE, TILE), table_ref[head, 0], WIDE)
            for bucket in range(1, BUCKETS):
                tile = jnp.where(marks == bucket, table_ref[head, bucket], tile)
            tiles.append(tile)
        for down in range((2 * slots - block) // TILE):
            for across in range(block // TILE):
                shift = down - (slots - block) // TILE - across
                if abs(shift) < 2:
                    tile = tiles[shift + 1]
                else:
                    far = table_ref[head, BUCKETS - 1 if shift > 0 else BUCKETS // 2 - 1]
                    tile = jnp.full((TILE, TILE), far, WIDE)
                out_ref[head, down * TILE : (down + 1) * TILE, across * TILE : (across + 1) * TILE] = tile


def bias_master(table, slots):
    heads = table.shape[0]
    shape = (heads, 2 * slots - QUERY_BLOCK, QUERY_BLOCK)
    return pl.pallas_call(
        functools.partial(bias_kernel, slots=slots, heads=heads),
        out_shape=jax.ShapeDtypeStruct(shape, WIDE),
        in_specs=[whole(pltpu.SMEM)],
        out_specs=whole(),
        compiler_params=pltpu.CompilerParams(vmem_limit_bytes=VMEM_LIMIT),
        cost_estimate=lasting(2),
        name="bias_master",
    )(table)


def whole(memory=pltpu.VMEM):
    return pl.BlockSpec(memory_space=memory)


def attend_forward(meta, rows_in, bias, slots, heads):
    width, block = heads * DK, QUERY_BLOCK
    return pl.pallas_call(
        functools.partial(forward_kernel, slots=slots, heads=heads),
        out_shape=(
            jax.ShapeDtypeStruct((slots, width), LOW),
            jax.ShapeDtypeStruct((8, slots), WIDE),
            jax.ShapeDtypeStruct((8, 128), WIDE),
        ),
        in_specs=[whole(pltpu.SMEM), whole(), whole()],
        out_specs=(whole(), whole(), whole()),
        scratch_shapes=[
            pltpu.VMEM((width, slots), WIDE),
            pltpu.VMEM((slots, block), jnp.int32),
        ],
        compiler_params=pltpu.CompilerParams(vmem_limit_bytes=VMEM_LIMIT),
        cost_estimate=lasting(10),
        name="attend_forward",
    )(meta, rows_in, bias)


def attend_backward(meta, rows_in, grad_in, log_total, bias, slots, heads):
    width, block = heads * DK, QUERY_BLOCK
    return pl.pallas_call(
        functools.partial(backward_kernel, slots=slots, heads=heads),
        out_shape=(
            jax.ShapeDtypeStruct((slots, 3 * width), LOW),
            jax.ShapeDtypeStruct((8, 128), WIDE),
        ),
        in_specs=[whole(pltpu.SMEM), whole(), whole(), whole(), whole()],
        out_specs=(whole(), whole()),
        scratch_shapes=[
            pltpu.VMEM((width, slots), WIDE),
            pltpu.VMEM((slots, block), jnp.int32),
            pltpu.VMEM((2 * slots - block, block), WIDE),
            pltpu.VMEM((slots, 2 * DK), WIDE),
        ],
        compiler_params=pltpu.CompilerParams(vmem_limit_bytes=VMEM_LIMIT),
        cost_estimate=lasting(15),
        name="attend_backward",
    )(meta, rows_in, grad_in, log_total, bias)


def gelu_with_slope(value):
    scale = math.sqrt(2.0 / math.pi)
    square = value * value
    bend = jnp.tanh(scale * (value + 0.044715 * value * square))
    active = 0.5 * value * (1.0 + bend)
    slope = 0.5 * (1.0 + bend) + 0.5 * value * (1.0 - bend * bend) * (scale * (1.0 + 3 * 0.044715 * square))
    return active, slope


def ffn_kernel(
    place_ref, rows_ref, grad_ref, *refs, count, units, tile
):
    gates, ups, downs = (refs[n * count : (n + 1) * count] for n in range(3))
    product_ref, both_ref, terms_ref = refs[3 * count :]
    depth = gates[0].shape[0]
    spans = [pl.ds(pl.multiple_of((place_ref[0] ^ n) * depth, depth), depth) for n in range(count)]

    def step(index, carry):
        rows = pl.ds(pl.multiple_of(index * tile, tile), tile)
        def columns_of(source, pieces):
            return sum(
                contract(source[rows, span], piece[...], 1, 0) for span, piece in zip(spans, pieces, strict=True)
            )

        gate_pre, upward = columns_of(rows_ref, gates), columns_of(rows_ref, ups)
        grad_product = columns_of(grad_ref, downs)
        active, slope = gelu_with_slope(gate_pre)
        product_ref[rows, :] = (active * upward).astype(LOW)
        both_ref[rows, :units] = (grad_product * upward * slope).astype(LOW)
        both_ref[rows, units:] = (grad_product * active).astype(LOW)
        for span, gate, up in zip(spans, gates, ups, strict=True):
            terms = contract(both_ref[rows, :units], gate[...], 1, 1)
            terms_ref[rows, span] = (terms + contract(both_ref[rows, units:], up[...], 1, 1)).astype(LOW)
        return carry

    lax.fori_loop(0, rows_ref.shape[0] // tile, step, 0)


def ffn_both_ways(place, rows_in, grad_in, gates, ups, downs):
    slots, model = rows_in.shape
    units = downs[0].shape[1]
    return pl.pallas_call(
        functools.partial(ffn_kernel, count=len(downs), units=units, tile=256),
        out_shape=(
            jax.ShapeDtypeStruct((slots, units), LOW),
            jax.ShapeDtypeStruct((slots, 2 * units), LOW),
            jax.ShapeDtypeStruct((slots, model), LOW),
        ),
        in_specs=[whole(pltpu.SMEM)] + [whole()] * (2 + 3 * len(downs)),
        out_specs=(whole(), whole(), whole()),
        compiler_params=pltpu.CompilerParams(vmem_limit_bytes=VMEM_LIMIT),
        cost_estimate=lasting(19),
        name="ffn_both_ways",
    )(place, rows_in, grad_in, *gates, *ups, *downs)


def ffn_out_kernel(place_ref, product_ref, *refs):
    pieces, terms_ref = refs[:-1], refs[-1]
    depth = pieces[0].shape[0]
    for n, piece in enumerate(pieces):
        span = pl.ds(pl.multiple_of((place_ref[0] ^ n) * depth, depth), depth)
        terms_ref[:, span] = contract(product_ref[...], piece[...], 1, 1).astype(LOW)


def ffn_out(place, product, pieces):
    slots, units = product.shape
    model = pieces[0].shape[0] * len(pieces)
    return pl.pallas_call(
        ffn_out_kernel,
        out_shape=jax.ShapeDtypeStruct((slots, model), LOW),
        in_specs=[whole(pltpu.SMEM)] + [whole()] * (1 + len(pieces)),
        out_specs=whole(),
        compiler_params=pltpu.CompilerParams(vmem_limit_bytes=VMEM_LIMIT),
        cost_estimate=lasting(5),
        name="ffn_out",
    )(place, product, *pieces)


def shards(
    tokens,
    out_grad,
    lengths,
    w_query,
    w_key,
    w_value,
    w_out,
    w_gate,
    w_up,
    w_down,
    gain_attn,
    gain_ffn,
    bias_table,
    clip_limit,
):
    groups, count, cores = (lax.axis_size(name) for name in ("fsdp", "ctx", "tp"))
    assert cores == 2
    group, here, core = (lax.axis_index(name) for name in ("fsdp", "ctx", "tp"))
    half = tokens.shape[1] // cores
    slots = tokens.shape[1] * count
    heads = bias_table.shape[0] // count
    head_width = heads * DK
    unit_width = w_gate.shape[1] // count
    weight_rows = w_query.shape[0]

    def flip(value, mask):
        return lax.ppermute(value, "fsdp", [(i, i ^ mask) for i in range(groups)])

    def swap(value):
        return lax.ppermute(value, "tp", [(0, 1), (1, 0)])

    def spread(parts, width):
        blocks = [
            jnp.concatenate([p[:, n * width : (n + 1) * width] for p in parts], axis=1) for n in range(count)
        ]
        return lax.all_to_all(jnp.concatenate(blocks, axis=0), "ctx", 0, 0, tiled=True)

    def return_rows(block):
        return lax.all_to_all(block, "ctx", 0, 0, tiled=True)

    def collect(rows, width):
        blocks = [rows[n * weight_rows : (n + 1) * weight_rows] for n in range(count)]
        return [
            jnp.concatenate([b[:, at : at + width] for b in blocks], axis=1).astype(WIDE)
            for at in range(0, rows.shape[1], width)
        ]

    def pieces_of(block):
        return [block] + [flip(block, n) for n in range(1, groups)]

    def assemble(pieces):
        rows = pieces[0].shape[0]
        result = jnp.zeros((groups * rows, pieces[0].shape[1]), LOW)
        for n, piece in enumerate(pieces):
            mask, start, part = piece if isinstance(piece, tuple) else (n, 0, piece)
            result = lax.dynamic_update_slice_in_dim(result, part, (group ^ mask) * rows + start, 0)
        return result

    def gather_quickly(block):
        if groups != 4:
            pieces = pieces_of(block)
            return assemble(pieces), pieces[-1]
        middle = block.shape[0] // 2
        first, second = flip(block, 1), flip(block, 2)
        low, high = flip(first[:middle], 2), flip(second[middle:], 1)
        return assemble([block, first, second, (3, 0, low), (3, middle, high)]), second

    def reduce_weights(terms):
        rows = terms.shape[0] // groups

        def block(mask):
            return lax.dynamic_slice_in_dim(terms, (group ^ mask) * rows, rows, 0)

        total = block(0).astype(WIDE)
        for mask in range(1, groups):
            total = total + flip(block(mask), mask).astype(WIDE)
        return total.astype(LOW)

    def after(value, *earlier):
        return lax.optimization_barrier((value, *earlier))[0]

    def together(*values):
        return lax.optimization_barrier(values)

    def gather_rows(piece):
        return lax.all_gather(piece, ("ctx", "tp"), axis=0, tiled=True)

    def reduce_rows(terms):
        return lax.psum_scatter(terms.astype(LOW), ("ctx", "tp"), scatter_dimension=0, tiled=True).astype(WIDE)

    def feed_forward(place, rows_in, grad_in, gate, up, down):
        if unit_width % 128 == 0:
            return ffn_both_ways(place, rows_in, grad_in, gate, up, down)
        gate, up, down = (assemble(pieces) for pieces in (gate, up, down))
        upward = contract(rows_in, up, 1, 0)
        active, slope = gelu_with_slope(contract(rows_in, gate, 1, 0))
        grad_product = contract(grad_in, down, 1, 0)
        product = (active * upward).astype(LOW)
        both = jnp.concatenate([grad_product * upward * slope, grad_product * active], axis=1).astype(LOW)
        terms = contract(both[:, :unit_width], gate, 1, 1) + contract(both[:, unit_width:], up, 1, 1)
        return product, both, terms.astype(LOW)

    def feed_forward_out(place, product, down):
        if unit_width % 128 == 0:
            return ffn_out(place, product, down)
        return contract(product, assemble(down), 1, 1).astype(LOW)

    def both_cores(piece):
        other = swap(piece)
        return jnp.where(
            core == 0, jnp.concatenate([piece, other], axis=0), jnp.concatenate([other, piece], axis=0)
        )

    def own_rows(value):
        return lax.dynamic_slice_in_dim(value[0], core * half, half, 0)

    def inverse_norm(value):
        return lax.rsqrt(jnp.mean(value * value, axis=-1, keepdims=True) + EPSILON)

    def norm_back(value, inverse, grad):
        along = jnp.mean(grad * value, axis=-1, keepdims=True)
        return inverse * grad - value * (inverse * inverse * inverse * along)

    ends = (lengths[0, 0], lengths[0, 0] + lengths[0, 1])
    meta = jnp.stack(ends).astype(jnp.int32)
    attn_gain = gain_attn.astype(WIDE)[:, None]
    ffn_gain = gain_ffn.astype(WIDE)[:, None]

    def scaled(weight, gain):
        return (weight.astype(WIDE) * gain).astype(LOW)

    query_key_value = [scaled(w, attn_gain) for w in (w_query, w_key, w_value)]
    inputs = own_rows(tokens).astype(WIDE)
    inverse_one = inverse_norm(inputs)
    row_place = (here * cores + core) * half + jnp.arange(half, dtype=jnp.int32)
    row_valid = (row_place < ends[1])[:, None]
    grad_out = jnp.where(row_valid, own_rows(out_grad).astype(WIDE), 0.0)
    my_table = lax.dynamic_slice_in_dim(bias_table, here * heads, heads, 0).astype(WIDE)

    bias = bias_master(my_table, slots)
    attn_mine = after(spread(query_key_value, head_width), bias)
    normed_rows = gather_rows(after((inputs * inverse_one).astype(LOW), attn_mine))
    attn_columns, arrived = gather_quickly(attn_mine)
    out_mine = spread([after(w_out, attn_mine)], head_width)
    normed = after(normed_rows, attn_columns, out_mine)
    out_pieces = pieces_of(after(out_mine, attn_columns))
    grad_rows = gather_rows(after(grad_out.astype(LOW), arrived))

    projected = contract(normed, attn_columns, 1, 0).astype(LOW)
    gate_mine = spread([scaled(after(w_gate, normed), ffn_gain)], unit_width)
    mixed, log_total, peaks = attend_forward(meta, projected, bias, slots, heads)
    branch_terms = contract(mixed, assemble(out_pieces), 1, 1).astype(LOW)
    branch_terms = after(branch_terms, gate_mine, grad_rows)
    up_mine = spread([scaled(after(w_up, gate_mine), ffn_gain)], unit_width)
    down_mine = spread([after(w_down, up_mine)], unit_width)
    gate_pieces = pieces_of(gate_mine)
    up_pieces = pieces_of(after(up_mine, *gate_pieces))
    branch = after(reduce_rows(branch_terms), down_mine, *up_pieces)
    down_pieces = pieces_of(after(down_mine, *up_pieces))
    hidden = inputs + branch
    inverse_two = inverse_norm(hidden)
    normed_ffn = gather_rows((hidden * inverse_two).astype(LOW))

    def sum_groups(left, right):
        return reduce_weights(contract(left, right, 0, 0).astype(LOW))

    place = group.astype(jnp.int32)[None]
    product, grad_both, ffn_terms = feed_forward(place, normed_ffn, grad_rows, gate_pieces, up_pieces, down_pieces)
    grad_normed_ffn = reduce_rows(ffn_terms)
    down_sum = sum_groups(after(grad_rows, ffn_terms), product)
    gate_up_terms = contract(after(normed_ffn, ffn_terms), grad_both, 0, 0).astype(LOW)
    out_terms = feed_forward_out(place, after(product, ffn_terms), down_pieces)
    gate_up_sum = reduce_weights(gate_up_terms)
    grad_normed_ffn = after(grad_normed_ffn, down_sum, gate_up_terms, out_terms)
    grad_hidden = grad_out + norm_back(hidden, inverse_two, grad_normed_ffn)
    branch_low = grad_hidden.astype(LOW)
    branch_rows, down_back, gate_up_sum = together(
        gather_rows(branch_low), return_rows(after(down_sum, branch_low)), gate_up_sum
    )

    grad_mixed = contract(branch_rows, assemble(out_pieces), 1, 0).astype(LOW)
    ffn_out_sum = reduce_rows(after(out_terms, branch_rows))
    grad_projected, table_terms = attend_backward(
        meta, projected, grad_mixed, log_total, bias, slots, heads
    )
    out_sum = sum_groups(branch_rows, after(mixed, grad_mixed))
    grad_projected, out_sum = together(grad_projected, out_sum)
    attn_terms = contract(normed, grad_projected, 0, 0).astype(LOW)
    attn_sum = reduce_weights(attn_terms)
    grad_normed = reduce_rows(contract(after(grad_projected, attn_terms), attn_columns, 1, 1))
    gate_up_back = return_rows(after(gate_up_sum, grad_mixed))
    gate_up_back, out_sum = together(gate_up_back, out_sum)
    attn_sum, out_back = together(attn_sum, return_rows(out_sum))
    attn_back = return_rows(attn_sum)
    grad_query_w, grad_key_w, grad_value_w = collect(attn_back, head_width)
    (grad_out_w,) = collect(out_back, head_width)
    (grad_down,) = collect(down_back, unit_width)
    grad_gate_w, grad_up_w = collect(gate_up_back, unit_width)
    mixed_out = both_cores((hidden + ffn_out_sum).astype(LOW))[None]
    grad_tokens = both_cores((grad_hidden + norm_back(inputs, inverse_one, grad_normed)).astype(LOW))[None]

    def gain_terms(weights, grads):
        return sum(jnp.sum(w.astype(WIDE) * g, axis=1) for w, g in zip(weights, grads, strict=True))

    gain_grads = jnp.stack(
        [
            gain_terms((w_query, w_key, w_value), (grad_query_w, grad_key_w, grad_value_w)),
            gain_terms((w_gate, w_up), (grad_gate_w, grad_up_w)),
        ]
    )
    gain_grads = gain_grads + swap(gain_grads)

    table_terms = after(table_terms, attn_sum)
    small = jnp.concatenate([table_terms[:heads, :BUCKETS], peaks[:heads, :1]], axis=1)
    blank = jnp.concatenate([jnp.zeros((1, BUCKETS), WIDE), jnp.full((1, 1), NEGATIVE, WIDE)], axis=1)
    is_sum = jnp.arange(BUCKETS + 1)[None, :] < BUCKETS
    small = jnp.where(
        (jnp.arange(count * heads) // heads == here)[:, None],
        jnp.tile(small, (count, 1)),
        blank,
    )

    def merge(first, second):
        return jnp.where(is_sum, first + second, jnp.maximum(first, second))

    mask = 1
    while mask < groups:
        small = merge(small, flip(small, mask))
        mask *= 2
    mask = 1
    while mask < count:
        small = merge(small, lax.ppermute(small, "ctx", [(i, i ^ mask) for i in range(count)]))
        mask *= 2
    grad_table, head_peaks = small[:, :BUCKETS], small[:, BUCKETS]
    factor = jnp.sqrt(clip_limit / jnp.maximum(head_peaks, clip_limit))
    factor_row = jnp.repeat(factor, DK)[None, :]

    def clipped(weight):
        return (weight.astype(WIDE) * factor_row).astype(LOW)

    return (
        mixed_out,
        grad_tokens,
        grad_query_w * attn_gain,
        grad_key_w * attn_gain,
        grad_value_w * attn_gain,
        grad_out_w,
        grad_gate_w * ffn_gain,
        grad_up_w * ffn_gain,
        grad_down,
        gain_grads[0],
        gain_grads[1],
        grad_table,
        head_peaks,
        clipped(w_query),
        clipped(w_key),
    )


def solution(mesh):
    rows, weight, gain = P("fsdp", "ctx", None), P(("fsdp", "ctx"), "tp"), P(("fsdp", "ctx"))
    return jax.shard_map(
        shards,
        mesh=mesh,
        in_specs=(rows, rows, P("fsdp", None)) + (weight,) * 7 + (gain, gain, P("tp", None), P("tp")),
        out_specs=(rows, rows) + (weight,) * 7 + (gain, gain, P("tp", None), P("tp"), weight, weight),
        check_vma=False,
    )
```

```python
import functools
import math

import jax
import jax.numpy as jnp
from jax import lax
from jax.experimental import pallas as pl
from jax.experimental.pallas import tpu as pltpu
from jax.sharding import PartitionSpec as P

DK = 64
BUCKETS = 32
THRESHOLDS = (12, 16, 23, 32, 46, 64, 91)
NEGATIVE = -1e30
EPSILON = 1e-06
QUERY_BLOCK = 256
TILE = 128
VMEM_LIMIT = 48 * 1024 * 1024
LOW = jnp.bfloat16
WIDE = jnp.float32


def lasting(micros):
    return pl.CostEstimate(flops=int(micros * 1.1e9), bytes_accessed=int(micros * 3.3e6), transcendentals=0)


def bucket_of(offset):
    distance = jnp.abs(offset)
    beyond = 8 + sum(((distance >= threshold).astype(jnp.int32) for threshold in THRESHOLDS))
    within = jnp.where(distance < 8, distance, beyond)
    return within + jnp.where(offset > 0, BUCKETS // 2, 0)


def contract(left, right, left_dim, right_dim):
    return lax.dot_general(
        left, right, (((left_dim,), (right_dim,)), ((), ())), preferred_element_type=WIDE
    )


def segments_down(meta_ref, shape):
    place = lax.broadcasted_iota(jnp.int32, shape, 0)
    return (place >= meta_ref[0]).astype(jnp.int32) + (place >= meta_ref[1]).astype(jnp.int32)


def segments_across(meta_ref, first, width):
    place = first + lax.broadcasted_iota(jnp.int32, (1, width), 1)
    return (place >= meta_ref[0]).astype(jnp.int32) + (place >= meta_ref[1]).astype(jnp.int32)


def forward_kernel(
    meta_ref, rows_ref, bias_ref, mixed_ref, log_ref, peak_ref, flip_ref, part_ref, *, slots, heads
):
    width, block = heads * DK, QUERY_BLOCK
    part_ref[...] = segments_down(meta_ref, (slots, block))
    log_ref[...] = jnp.zeros_like(log_ref)
    peak_ref[...] = jnp.full(peak_ref.shape, NEGATIVE, WIDE)
    for head in range(heads):
        at = head * DK
        keys = rows_ref[:, width + at : width + at + DK]
        queries_flip = rows_ref[:, at : at + DK].T
        values_flip = rows_ref[:, 2 * width + at : 2 * width + at + DK].T
        peak = jnp.full((1, block), NEGATIVE, WIDE)
        for step in range(slots // block):
            first = step * block
            across = segments_across(meta_ref, first, block)
            logits = contract(keys, queries_flip[:, first : first + block], 1, 0)
            logits = jnp.where(part_ref[...] == across, logits, NEGATIVE)
            tops = jnp.max(logits, axis=0, keepdims=True)
            peak = jnp.maximum(peak, jnp.where(across < 2, tops, NEGATIVE))
            start = slots - block - first
            scores = logits + bias_ref[head, start : start + slots, :]
            highest = jnp.max(scores, axis=0, keepdims=True)
            weights = jnp.exp(scores - highest)
            total = jnp.sum(weights, axis=0, keepdims=True)
            mixed = contract(values_flip, weights.astype(LOW), 1, 0)
            flip_ref[at : at + DK, first : first + block] = mixed / total
            log_ref[head : head + 1, first : first + block] = highest + jnp.log(total)
        peak_ref[head : head + 1, :] = jnp.broadcast_to(
            jnp.max(peak, axis=1, keepdims=True), (1, peak_ref.shape[1])
        )
    mixed_ref[...] = flip_ref[...].T.astype(LOW)


def backward_kernel(
    meta_ref,
    rows_ref,
    grad_ref,
    log_ref,
    bias_ref,
    out_ref,
    table_ref,
    flip_ref,
    part_ref,
    sums_ref,
    down_ref,
    *,
    slots,
    heads,
):
    width, block = heads * DK, QUERY_BLOCK
    part_ref[...] = segments_down(meta_ref, (slots, block))
    table_ref[...] = jnp.zeros_like(table_ref)
    lane = lax.broadcasted_iota(jnp.int32, (1, table_ref.shape[1]), 1)
    offsets = tile_offsets()
    marks = [bucket_of(offsets + shift * TILE) for shift in (-1, 0, 1)]
    for head in range(heads):
        at = head * DK
        queries = rows_ref[:, at : at + DK]
        keys = rows_ref[:, width + at : width + at + DK]
        values = rows_ref[:, 2 * width + at : 2 * width + at + DK]
        grads = grad_ref[:, at : at + DK]
        queries_flip, keys_flip, grads_flip = queries.T, keys.T, grads.T
        sums_ref[...] = jnp.zeros_like(sums_ref)
        for step in range(slots // block):
            first = step * block
            across = segments_across(meta_ref, first, block)
            start = slots - block - first
            logits = contract(keys, queries_flip[:, first : first + block], 1, 0)
            scores = logits + bias_ref[head, start : start + slots, :]
            scores = scores - log_ref[head : head + 1, first : first + block]
            chance = jnp.exp(jnp.where(part_ref[...] == across, scores, NEGATIVE))
            grad_chance = contract(values, grads_flip[:, first : first + block], 1, 0)
            delta = jnp.sum(chance * grad_chance, axis=0, keepdims=True)
            grad_scores = chance * (grad_chance - delta)
            sums_ref[start : start + slots, :] += grad_scores
            rounded = grad_scores.astype(LOW)
            grad_keys = contract(rounded, queries[first : first + block, :], 1, 0)
            grad_values = contract(chance.astype(LOW), grads[first : first + block, :], 1, 0)
            if step == 0:
                down_ref[:, :DK] = grad_keys
                down_ref[:, DK:] = grad_values
            else:
                down_ref[:, :DK] += grad_keys
                down_ref[:, DK:] += grad_values
            flip_ref[at : at + DK, first : first + block] = contract(keys_flip, rounded, 1, 0)
        out_ref[:, width + at : width + at + DK] = down_ref[:, :DK].astype(LOW)
        out_ref[:, 2 * width + at : 2 * width + at + DK] = down_ref[:, DK:].astype(LOW)
        near = [jnp.zeros((TILE, TILE), WIDE) for _ in marks]
        far = [jnp.zeros((TILE, TILE), WIDE) for _ in range(2)]
        for down in range((2 * slots - block) // TILE):
            for across in range(block // TILE):
                shift = down - (slots - block) // TILE - across
                tile = sums_ref[down * TILE : (down + 1) * TILE, across * TILE : (across + 1) * TILE]
                if abs(shift) < 2:
                    near[shift + 1] = near[shift + 1] + tile
                else:
                    far[int(shift > 0)] = far[int(shift > 0)] + tile
        row = jnp.where(lane == BUCKETS // 2 - 1, jnp.sum(far[0]), 0.0)
        row = row + jnp.where(lane == BUCKETS - 1, jnp.sum(far[1]), 0.0)
        for bucket in range(BUCKETS):
            held = sum(
                jnp.where(mark == bucket, tile, 0.0) for mark, tile in zip(marks, near, strict=True)
            )
            row = row + jnp.where(lane == bucket, jnp.sum(held), 0.0)
        table_ref[head : head + 1, :] = row
    out_ref[:, :width] = flip_ref[...].T.astype(LOW)


def tile_offsets():
    return lax.broadcasted_iota(jnp.int32, (TILE, TILE), 0) - lax.broadcasted_iota(jnp.int32, (TILE, TILE), 1)


def bias_kernel(table_ref, out_ref, *, slots, heads):
    block = QUERY_BLOCK
    offsets = tile_offsets()
    buckets = [bucket_of(offsets + shift * TILE) for shift in (-1, 0, 1)]
    for head in range(heads):
        tiles = []
        for marks in buckets:
            tile = jnp.full((TILE, TILE), table_ref[head, 0], WIDE)
            for bucket in range(1, BUCKETS):
                tile = jnp.where(marks == bucket, table_ref[head, bucket], tile)
            tiles.append(tile)
        for down in range((2 * slots - block) // TILE):
            for across in range(block // TILE):
                shift = down - (slots - block) // TILE - across
                if abs(shift) < 2:
                    tile = tiles[shift + 1]
                else:
                    far = table_ref[head, BUCKETS - 1 if shift > 0 else BUCKETS // 2 - 1]
                    tile = jnp.full((TILE, TILE), far, WIDE)
                out_ref[head, down * TILE : (down + 1) * TILE, across * TILE : (across + 1) * TILE] = tile


def bias_master(table, slots):
    heads = table.shape[0]
    shape = (heads, 2 * slots - QUERY_BLOCK, QUERY_BLOCK)
    return pl.pallas_call(
        functools.partial(bias_kernel, slots=slots, heads=heads),
        out_shape=jax.ShapeDtypeStruct(shape, WIDE),
        in_specs=[whole(pltpu.SMEM)],
        out_specs=whole(),
        compiler_params=pltpu.CompilerParams(vmem_limit_bytes=VMEM_LIMIT),
        cost_estimate=lasting(2),
        name="bias_master",
    )(table)


def whole(memory=pltpu.VMEM):
    return pl.BlockSpec(memory_space=memory)


def attend_forward(meta, rows_in, bias, slots, heads):
    width, block = heads * DK, QUERY_BLOCK
    return pl.pallas_call(
        functools.partial(forward_kernel, slots=slots, heads=heads),
        out_shape=(
            jax.ShapeDtypeStruct((slots, width), LOW),
            jax.ShapeDtypeStruct((8, slots), WIDE),
            jax.ShapeDtypeStruct((8, 128), WIDE),
        ),
        in_specs=[whole(pltpu.SMEM), whole(), whole()],
        out_specs=(whole(), whole(), whole()),
        scratch_shapes=[
            pltpu.VMEM((width, slots), WIDE),
            pltpu.VMEM((slots, block), jnp.int32),
        ],
        compiler_params=pltpu.CompilerParams(vmem_limit_bytes=VMEM_LIMIT),
        cost_estimate=lasting(10),
        name="attend_forward",
    )(meta, rows_in, bias)


def attend_backward(meta, rows_in, grad_in, log_total, bias, slots, heads):
    width, block = heads * DK, QUERY_BLOCK
    return pl.pallas_call(
        functools.partial(backward_kernel, slots=slots, heads=heads),
        out_shape=(
            jax.ShapeDtypeStruct((slots, 3 * width), LOW),
            jax.ShapeDtypeStruct((8, 128), WIDE),
        ),
        in_specs=[whole(pltpu.SMEM), whole(), whole(), whole(), whole()],
        out_specs=(whole(), whole()),
        scratch_shapes=[
            pltpu.VMEM((width, slots), WIDE),
            pltpu.VMEM((slots, block), jnp.int32),
            pltpu.VMEM((2 * slots - block, block), WIDE),
            pltpu.VMEM((slots, 2 * DK), WIDE),
        ],
        compiler_params=pltpu.CompilerParams(vmem_limit_bytes=VMEM_LIMIT),
        cost_estimate=lasting(15),
        name="attend_backward",
    )(meta, rows_in, grad_in, log_total, bias)


def gelu_with_slope(value):
    scale = math.sqrt(2.0 / math.pi)
    square = value * value
    bend = jnp.tanh(scale * (value + 0.044715 * value * square))
    active = 0.5 * value * (1.0 + bend)
    slope = 0.5 * (1.0 + bend) + 0.5 * value * (1.0 - bend * bend) * (scale * (1.0 + 3 * 0.044715 * square))
    return active, slope


def ffn_kernel(
    place_ref, rows_ref, grad_ref, *refs, count, units, tile
):
    gates, ups, downs = (refs[n * count : (n + 1) * count] for n in range(3))
    product_ref, both_ref, terms_ref = refs[3 * count :]
    depth = gates[0].shape[0]
    spans = [pl.ds(pl.multiple_of((place_ref[0] ^ n) * depth, depth), depth) for n in range(count)]

    def step(index, carry):
        rows = pl.ds(pl.multiple_of(index * tile, tile), tile)
        def columns_of(source, pieces):
            return sum(
                contract(source[rows, span], piece[...], 1, 0) for span, piece in zip(spans, pieces, strict=True)
            )

        gate_pre, upward = columns_of(rows_ref, gates), columns_of(rows_ref, ups)
        grad_product = columns_of(grad_ref, downs)
        active, slope = gelu_with_slope(gate_pre)
        product_ref[rows, :] = (active * upward).astype(LOW)
        both_ref[rows, :units] = (grad_product * upward * slope).astype(LOW)
        both_ref[rows, units:] = (grad_product * active).astype(LOW)
        for span, gate, up in zip(spans, gates, ups, strict=True):
            terms = contract(both_ref[rows, :units], gate[...], 1, 1)
            terms_ref[rows, span] = (terms + contract(both_ref[rows, units:], up[...], 1, 1)).astype(LOW)
        return carry

    lax.fori_loop(0, rows_ref.shape[0] // tile, step, 0)


def ffn_both_ways(place, rows_in, grad_in, gates, ups, downs):
    slots, model = rows_in.shape
    units = downs[0].shape[1]
    return pl.pallas_call(
        functools.partial(ffn_kernel, count=len(downs), units=units, tile=256),
        out_shape=(
            jax.ShapeDtypeStruct((slots, units), LOW),
            jax.ShapeDtypeStruct((slots, 2 * units), LOW),
            jax.ShapeDtypeStruct((slots, model), LOW),
        ),
        in_specs=[whole(pltpu.SMEM)] + [whole()] * (2 + 3 * len(downs)),
        out_specs=(whole(), whole(), whole()),
        compiler_params=pltpu.CompilerParams(vmem_limit_bytes=VMEM_LIMIT),
        cost_estimate=lasting(19),
        name="ffn_both_ways",
    )(place, rows_in, grad_in, *gates, *ups, *downs)


def ffn_out_kernel(place_ref, product_ref, *refs):
    pieces, terms_ref = refs[:-1], refs[-1]
    depth = pieces[0].shape[0]
    for n, piece in enumerate(pieces):
        span = pl.ds(pl.multiple_of((place_ref[0] ^ n) * depth, depth), depth)
        terms_ref[:, span] = contract(product_ref[...], piece[...], 1, 1).astype(LOW)


def ffn_out(place, product, pieces):
    slots, units = product.shape
    model = pieces[0].shape[0] * len(pieces)
    return pl.pallas_call(
        ffn_out_kernel,
        out_shape=jax.ShapeDtypeStruct((slots, model), LOW),
        in_specs=[whole(pltpu.SMEM)] + [whole()] * (1 + len(pieces)),
        out_specs=whole(),
        compiler_params=pltpu.CompilerParams(vmem_limit_bytes=VMEM_LIMIT),
        cost_estimate=lasting(5),
        name="ffn_out",
    )(place, product, *pieces)


def pack_kernel(gain_ref, *refs, count, scaled):
    parts, out_ref = refs[:-1], refs[-1]
    rows, width = parts[0].shape[0], parts[0].shape[1] // count
    for n, (part, scale) in enumerate(zip(parts, scaled, strict=True)):
        for block in range(count):
            piece = part[:, block * width : (block + 1) * width]
            if scale:
                piece = (piece.astype(WIDE) * gain_ref[...]).astype(LOW)
            out_ref[block * rows : (block + 1) * rows, n * width : (n + 1) * width] = piece


def pack(gain, parts, scaled, count):
    rows, columns = parts[0].shape
    return pl.pallas_call(
        functools.partial(pack_kernel, count=count, scaled=scaled),
        out_shape=jax.ShapeDtypeStruct((count * rows, len(parts) * columns // count), LOW),
        in_specs=[whole()] * (1 + len(parts)),
        out_specs=whole(),
        compiler_params=pltpu.CompilerParams(vmem_limit_bytes=VMEM_LIMIT),
        cost_estimate=lasting(2),
        name="pack",
    )(gain, *parts)


def shards(
    tokens,
    out_grad,
    lengths,
    w_query,
    w_key,
    w_value,
    w_out,
    w_gate,
    w_up,
    w_down,
    gain_attn,
    gain_ffn,
    bias_table,
    clip_limit,
):
    groups, count, cores = (lax.axis_size(name) for name in ("fsdp", "ctx", "tp"))
    assert cores == 2
    group, here, core = (lax.axis_index(name) for name in ("fsdp", "ctx", "tp"))
    half = tokens.shape[1] // cores
    slots = tokens.shape[1] * count
    heads = bias_table.shape[0] // count
    head_width = heads * DK
    unit_width = w_gate.shape[1] // count
    weight_rows = w_query.shape[0]

    def flip(value, mask):
        return lax.ppermute(value, "fsdp", [(i, i ^ mask) for i in range(groups)])

    def swap(value):
        return lax.ppermute(value, "tp", [(0, 1), (1, 0)])

    def spread(parts, gain, scaled):
        if parts[0].shape[1] // count % 128 == 0:
            packed = pack(gain, parts, scaled, count)
        else:
            parts = [(p.astype(WIDE) * gain).astype(LOW) if s else p for p, s in zip(parts, scaled, strict=True)]
            width = parts[0].shape[1] // count
            packed = jnp.concatenate(
                [
                    jnp.concatenate([p[:, n * width : (n + 1) * width] for p in parts], axis=1)
                    for n in range(count)
                ],
                axis=0,
            )
        return lax.all_to_all(packed, "ctx", 0, 0, tiled=True)

    def return_rows(block):
        return lax.all_to_all(block, "ctx", 0, 0, tiled=True)

    def collect(rows, width):
        blocks = [rows[n * weight_rows : (n + 1) * weight_rows] for n in range(count)]
        return [
            jnp.concatenate([b[:, at : at + width] for b in blocks], axis=1).astype(WIDE)
            for at in range(0, rows.shape[1], width)
        ]

    def pieces_of(block):
        return [block] + [flip(block, n) for n in range(1, groups)]

    def assemble(pieces):
        rows = pieces[0].shape[0]
        result = jnp.zeros((groups * rows, pieces[0].shape[1]), LOW)
        for n, piece in enumerate(pieces):
            mask, start, part = piece if isinstance(piece, tuple) else (n, 0, piece)
            result = lax.dynamic_update_slice_in_dim(result, part, (group ^ mask) * rows + start, 0)
        return result

    def gather_quickly(block):
        if groups != 4:
            pieces = pieces_of(block)
            return assemble(pieces), pieces[-1]
        middle = block.shape[0] // 2
        first, second = flip(block, 1), flip(block, 2)
        low, high = flip(first[:middle], 2), flip(second[middle:], 1)
        return assemble([block, first, second, (3, 0, low), (3, middle, high)]), first, second

    def blocks_of(terms):
        rows = terms.shape[0] // groups
        return [lax.dynamic_slice_in_dim(terms, (group ^ n) * rows, rows, 0) for n in range(groups)]

    def flip_blocks(blocks):
        return [block if n == 0 else flip(block, n) for n, block in enumerate(blocks)]

    def sum_of(blocks):
        return sum(block.astype(WIDE) for block in blocks).astype(LOW)

    def reduce_weights(terms):
        return sum_of(flip_blocks(blocks_of(terms)))

    def after(value, *earlier):
        return lax.optimization_barrier((value, *earlier))[0]

    def together(*values):
        return lax.optimization_barrier(values)

    def gather_rows(piece):
        return lax.all_gather(piece, ("ctx", "tp"), axis=0, tiled=True)

    def reduce_rows(terms):
        return lax.psum_scatter(terms.astype(LOW), ("ctx", "tp"), scatter_dimension=0, tiled=True).astype(WIDE)

    def feed_forward(place, rows_in, grad_in, gate, up, down):
        if unit_width % 128 == 0:
            return ffn_both_ways(place, rows_in, grad_in, gate, up, down)
        gate, up, down = (assemble(pieces) for pieces in (gate, up, down))
        upward = contract(rows_in, up, 1, 0)
        active, slope = gelu_with_slope(contract(rows_in, gate, 1, 0))
        grad_product = contract(grad_in, down, 1, 0)
        product = (active * upward).astype(LOW)
        both = jnp.concatenate([grad_product * upward * slope, grad_product * active], axis=1).astype(LOW)
        terms = contract(both[:, :unit_width], gate, 1, 1) + contract(both[:, unit_width:], up, 1, 1)
        return product, both, terms.astype(LOW)

    def feed_forward_out(place, product, down):
        if unit_width % 128 == 0:
            return ffn_out(place, product, down)
        return contract(product, assemble(down), 1, 1).astype(LOW)

    def both_cores(piece):
        other = swap(piece)
        return jnp.where(
            core == 0, jnp.concatenate([piece, other], axis=0), jnp.concatenate([other, piece], axis=0)
        )

    def own_rows(value):
        return lax.dynamic_slice_in_dim(value[0], core * half, half, 0)

    def inverse_norm(value):
        return lax.rsqrt(jnp.mean(value * value, axis=-1, keepdims=True) + EPSILON)

    def norm_back(value, inverse, grad):
        along = jnp.mean(grad * value, axis=-1, keepdims=True)
        return inverse * grad - value * (inverse * inverse * inverse * along)

    ends = (lengths[0, 0], lengths[0, 0] + lengths[0, 1])
    meta = jnp.stack(ends).astype(jnp.int32)
    attn_gain = gain_attn.astype(WIDE)[:, None]
    ffn_gain = gain_ffn.astype(WIDE)[:, None]

    inputs = own_rows(tokens).astype(WIDE)
    inverse_one = inverse_norm(inputs)
    row_place = (here * cores + core) * half + jnp.arange(half, dtype=jnp.int32)
    row_valid = (row_place < ends[1])[:, None]
    grad_out = jnp.where(row_valid, own_rows(out_grad).astype(WIDE), 0.0)
    my_table = lax.dynamic_slice_in_dim(bias_table, here * heads, heads, 0).astype(WIDE)

    bias = bias_master(my_table, slots)
    attn_mine = after(
        spread([w_query, w_key, w_value, w_out], attn_gain, (True, True, True, False)), bias
    )
    normed_rows = gather_rows(after((inputs * inverse_one).astype(LOW), attn_mine))
    all_columns, *arrived = gather_quickly(attn_mine)
    attn_columns, out_columns = all_columns[:, : 3 * head_width], all_columns[:, 3 * head_width :]
    gate_mine = spread([after(w_gate, attn_mine)], ffn_gain, (True,))
    normed = after(normed_rows, all_columns, gate_mine)
    grad_rows = gather_rows(after(grad_out.astype(LOW), *arrived))

    projected = contract(normed, attn_columns, 1, 0).astype(LOW)
    gate_pieces = pieces_of(after(gate_mine, all_columns))
    mixed, log_total, peaks = attend_forward(meta, projected, bias, slots, heads)
    branch_terms = contract(mixed, out_columns, 1, 1).astype(LOW)
    up_mine = spread([after(w_up, normed)], ffn_gain, (True,))
    branch_terms = after(branch_terms, grad_rows, up_mine, *gate_pieces)
    down_mine = spread([after(w_down, up_mine)], ffn_gain, (False,))
    up_pieces = pieces_of(after(up_mine, *gate_pieces))
    branch = after(reduce_rows(branch_terms), down_mine, *up_pieces)
    down_pieces = pieces_of(after(down_mine, *up_pieces))
    hidden = inputs + branch
    inverse_two = inverse_norm(hidden)
    normed_ffn = gather_rows((hidden * inverse_two).astype(LOW))

    place = group.astype(jnp.int32)[None]
    product, grad_both, ffn_terms = feed_forward(place, normed_ffn, grad_rows, gate_pieces, up_pieces, down_pieces)
    grad_normed_ffn = reduce_rows(ffn_terms)
    out_terms = feed_forward_out(place, after(product, ffn_terms), down_pieces)
    gate_terms = contract(after(normed_ffn, ffn_terms), grad_both[:, :unit_width], 0, 0).astype(LOW)
    up_terms = contract(after(normed_ffn, ffn_terms), grad_both[:, unit_width:], 0, 0).astype(LOW)
    down_terms = contract(after(grad_rows, ffn_terms), product, 0, 0).astype(LOW)
    first_sum = reduce_weights(gate_terms)
    grad_normed_ffn = after(grad_normed_ffn, first_sum, up_terms, down_terms, out_terms)
    grad_hidden = grad_out + norm_back(hidden, inverse_two, grad_normed_ffn)
    branch_low = grad_hidden.astype(LOW)
    cut = unit_width * 3 // 5
    second_blocks = [
        jnp.concatenate(pair, axis=1)
        for pair in zip(blocks_of(up_terms), blocks_of(down_terms[:, :cut]), strict=True)
    ]
    second_sum = sum_of(flip_blocks(second_blocks))
    gathered = gather_rows(branch_low)
    branch_rows, second_sum = together(gathered, second_sum)
    ffn_out_sum = reduce_rows(after(out_terms, gathered))

    grad_mixed = contract(branch_rows, out_columns, 1, 0).astype(LOW)
    units = jnp.concatenate([first_sum, second_sum], axis=1)
    units = after(units, grad_mixed)
    grad_projected, table_terms = attend_backward(
        meta, projected, grad_mixed, log_total, bias, slots, heads
    )
    units_back = return_rows(units)
    third_blocks = blocks_of(after(down_terms[:, cut:], second_sum))
    out_blocks = blocks_of(contract(branch_rows, after(mixed, grad_mixed), 0, 0).astype(LOW))
    third_sum = sum_of(
        flip_blocks([jnp.concatenate(pair, axis=1) for pair in zip(out_blocks, third_blocks, strict=True)])
    )
    grad_projected, third_sum = together(grad_projected, third_sum)
    attn_terms = contract(normed, grad_projected, 0, 0).astype(LOW)
    attn_sum = reduce_weights(attn_terms)
    grad_normed = reduce_rows(contract(after(grad_projected, attn_terms), attn_columns, 1, 1))
    attn_sum, units_back = together(attn_sum, units_back)
    attn_back = return_rows(jnp.concatenate([attn_sum, third_sum], axis=1))
    grad_query_w, grad_key_w, grad_value_w, grad_out_w = collect(attn_back[:, : 4 * head_width], head_width)
    grad_gate_w, grad_up_w = collect(units_back[:, : 2 * unit_width], unit_width)
    (grad_down,) = collect(
        jnp.concatenate([units_back[:, 2 * unit_width :], attn_back[:, 4 * head_width :]], axis=1), unit_width
    )
    mixed_out = both_cores((hidden + ffn_out_sum).astype(LOW))[None]
    grad_tokens = both_cores((grad_hidden + norm_back(inputs, inverse_one, grad_normed)).astype(LOW))[None]

    def gain_terms(weights, grads):
        return sum(jnp.sum(w.astype(WIDE) * g, axis=1) for w, g in zip(weights, grads, strict=True))

    gain_grads = jnp.stack(
        [
            gain_terms((w_query, w_key, w_value), (grad_query_w, grad_key_w, grad_value_w)),
            gain_terms((w_gate, w_up), (grad_gate_w, grad_up_w)),
        ]
    )
    gain_grads = gain_grads + swap(gain_grads)

    table_terms = after(table_terms, attn_sum)
    small = jnp.concatenate([table_terms[:heads, :BUCKETS], peaks[:heads, :1]], axis=1)
    blank = jnp.concatenate([jnp.zeros((1, BUCKETS), WIDE), jnp.full((1, 1), NEGATIVE, WIDE)], axis=1)
    is_sum = jnp.arange(BUCKETS + 1)[None, :] < BUCKETS
    small = jnp.where(
        (jnp.arange(count * heads) // heads == here)[:, None],
        jnp.tile(small, (count, 1)),
        blank,
    )

    def merge(first, second):
        return jnp.where(is_sum, first + second, jnp.maximum(first, second))

    mask = 1
    while mask < groups:
        small = merge(small, flip(small, mask))
        mask *= 2
    mask = 1
    while mask < count:
        small = merge(small, lax.ppermute(small, "ctx", [(i, i ^ mask) for i in range(count)]))
        mask *= 2
    grad_table, head_peaks = small[:, :BUCKETS], small[:, BUCKETS]
    factor = jnp.sqrt(clip_limit / jnp.maximum(head_peaks, clip_limit))
    factor_row = jnp.repeat(factor, DK)[None, :]

    def clipped(weight):
        return (weight.astype(WIDE) * factor_row).astype(LOW)

    return (
        mixed_out,
        grad_tokens,
        grad_query_w * attn_gain,
        grad_key_w * attn_gain,
        grad_value_w * attn_gain,
        grad_out_w,
        grad_gate_w * ffn_gain,
        grad_up_w * ffn_gain,
        grad_down,
        gain_grads[0],
        gain_grads[1],
        grad_table,
        head_peaks,
        clipped(w_query),
        clipped(w_key),
    )


def solution(mesh):
    rows, weight, gain = P("fsdp", "ctx", None), P(("fsdp", "ctx"), "tp"), P(("fsdp", "ctx"))
    return jax.shard_map(
        shards,
        mesh=mesh,
        in_specs=(rows, rows, P("fsdp", None)) + (weight,) * 7 + (gain, gain, P("tp", None), P("tp")),
        out_specs=(rows, rows) + (weight,) * 7 + (gain, gain, P("tp", None), P("tp"), weight, weight),
        check_vma=False,
    )
```

```python
import functools
import math

import jax
import jax.numpy as jnp
from jax import lax
from jax.experimental import pallas as pl
from jax.experimental.pallas import tpu as pltpu
from jax.sharding import PartitionSpec as P

DK = 64
BUCKETS = 32
THRESHOLDS = (12, 16, 23, 32, 46, 64, 91)
NEGATIVE = -1e30
EPSILON = 1e-06
QUERY_BLOCK = 256
TILE = 128
VMEM_LIMIT = 48 * 1024 * 1024
LOW = jnp.bfloat16
WIDE = jnp.float32


def lasting(micros):
    return pl.CostEstimate(flops=int(micros * 1.1e9), bytes_accessed=int(micros * 3.3e6), transcendentals=0)


def bucket_of(offset):
    distance = jnp.abs(offset)
    beyond = 8 + sum(((distance >= threshold).astype(jnp.int32) for threshold in THRESHOLDS))
    within = jnp.where(distance < 8, distance, beyond)
    return within + jnp.where(offset > 0, BUCKETS // 2, 0)


def contract(left, right, left_dim, right_dim):
    return lax.dot_general(
        left, right, (((left_dim,), (right_dim,)), ((), ())), preferred_element_type=WIDE
    )


def segments_down(meta_ref, shape):
    place = lax.broadcasted_iota(jnp.int32, shape, 0)
    return (place >= meta_ref[0]).astype(jnp.int32) + (place >= meta_ref[1]).astype(jnp.int32)


def segments_across(meta_ref, first, width):
    place = first + lax.broadcasted_iota(jnp.int32, (1, width), 1)
    return (place >= meta_ref[0]).astype(jnp.int32) + (place >= meta_ref[1]).astype(jnp.int32)


def forward_kernel(
    meta_ref, rows_ref, bias_ref, mixed_ref, log_ref, peak_ref, flip_ref, part_ref, *, slots, heads
):
    width, block = heads * DK, QUERY_BLOCK
    part_ref[...] = segments_down(meta_ref, (slots, block))
    log_ref[...] = jnp.zeros_like(log_ref)
    peak_ref[...] = jnp.full(peak_ref.shape, NEGATIVE, WIDE)
    for head in range(heads):
        at = head * DK
        keys = rows_ref[:, width + at : width + at + DK]
        queries_flip = rows_ref[:, at : at + DK].T
        values_flip = rows_ref[:, 2 * width + at : 2 * width + at + DK].T
        peak = jnp.full((1, block), NEGATIVE, WIDE)
        for step in range(slots // block):
            first = step * block
            across = segments_across(meta_ref, first, block)
            logits = contract(keys, queries_flip[:, first : first + block], 1, 0)
            logits = jnp.where(part_ref[...] == across, logits, NEGATIVE)
            tops = jnp.max(logits, axis=0, keepdims=True)
            peak = jnp.maximum(peak, jnp.where(across < 2, tops, NEGATIVE))
            start = slots - block - first
            scores = logits + bias_ref[head, start : start + slots, :]
            highest = jnp.max(scores, axis=0, keepdims=True)
            weights = jnp.exp(scores - highest)
            total = jnp.sum(weights, axis=0, keepdims=True)
            mixed = contract(values_flip, weights.astype(LOW), 1, 0)
            flip_ref[at : at + DK, first : first + block] = mixed / total
            log_ref[head : head + 1, first : first + block] = highest + jnp.log(total)
        peak_ref[head : head + 1, :] = jnp.broadcast_to(
            jnp.max(peak, axis=1, keepdims=True), (1, peak_ref.shape[1])
        )
    mixed_ref[...] = flip_ref[...].T.astype(LOW)


def backward_kernel(
    meta_ref,
    rows_ref,
    grad_ref,
    log_ref,
    bias_ref,
    out_ref,
    table_ref,
    flip_ref,
    part_ref,
    sums_ref,
    down_ref,
    *,
    slots,
    heads,
):
    width, block = heads * DK, QUERY_BLOCK
    part_ref[...] = segments_down(meta_ref, (slots, block))
    table_ref[...] = jnp.zeros_like(table_ref)
    lane = lax.broadcasted_iota(jnp.int32, (1, table_ref.shape[1]), 1)
    offsets = tile_offsets()
    marks = [bucket_of(offsets + shift * TILE) for shift in (-1, 0, 1)]
    for head in range(heads):
        at = head * DK
        queries = rows_ref[:, at : at + DK]
        keys = rows_ref[:, width + at : width + at + DK]
        values = rows_ref[:, 2 * width + at : 2 * width + at + DK]
        grads = grad_ref[:, at : at + DK]
        queries_flip, keys_flip, grads_flip = queries.T, keys.T, grads.T
        sums_ref[...] = jnp.zeros_like(sums_ref)
        for step in range(slots // block):
            first = step * block
            across = segments_across(meta_ref, first, block)
            start = slots - block - first
            logits = contract(keys, queries_flip[:, first : first + block], 1, 0)
            scores = logits + bias_ref[head, start : start + slots, :]
            scores = scores - log_ref[head : head + 1, first : first + block]
            chance = jnp.exp(jnp.where(part_ref[...] == across, scores, NEGATIVE))
            grad_chance = contract(values, grads_flip[:, first : first + block], 1, 0)
            delta = jnp.sum(chance * grad_chance, axis=0, keepdims=True)
            grad_scores = chance * (grad_chance - delta)
            sums_ref[start : start + slots, :] += grad_scores
            rounded = grad_scores.astype(LOW)
            grad_keys = contract(rounded, queries[first : first + block, :], 1, 0)
            grad_values = contract(chance.astype(LOW), grads[first : first + block, :], 1, 0)
            if step == 0:
                down_ref[:, :DK] = grad_keys
                down_ref[:, DK:] = grad_values
            else:
                down_ref[:, :DK] += grad_keys
                down_ref[:, DK:] += grad_values
            flip_ref[at : at + DK, first : first + block] = contract(keys_flip, rounded, 1, 0)
        out_ref[:, width + at : width + at + DK] = down_ref[:, :DK].astype(LOW)
        out_ref[:, 2 * width + at : 2 * width + at + DK] = down_ref[:, DK:].astype(LOW)
        near = [jnp.zeros((TILE, TILE), WIDE) for _ in marks]
        far = [jnp.zeros((TILE, TILE), WIDE) for _ in range(2)]
        for down in range((2 * slots - block) // TILE):
            for across in range(block // TILE):
                shift = down - (slots - block) // TILE - across
                tile = sums_ref[down * TILE : (down + 1) * TILE, across * TILE : (across + 1) * TILE]
                if abs(shift) < 2:
                    near[shift + 1] = near[shift + 1] + tile
                else:
                    far[int(shift > 0)] = far[int(shift > 0)] + tile
        row = jnp.where(lane == BUCKETS // 2 - 1, jnp.sum(far[0]), 0.0)
        row = row + jnp.where(lane == BUCKETS - 1, jnp.sum(far[1]), 0.0)
        for bucket in range(BUCKETS):
            held = sum(
                jnp.where(mark == bucket, tile, 0.0) for mark, tile in zip(marks, near, strict=True)
            )
            row = row + jnp.where(lane == bucket, jnp.sum(held), 0.0)
        table_ref[head : head + 1, :] = row
    out_ref[:, :width] = flip_ref[...].T.astype(LOW)


def tile_offsets():
    return lax.broadcasted_iota(jnp.int32, (TILE, TILE), 0) - lax.broadcasted_iota(jnp.int32, (TILE, TILE), 1)


def bias_kernel(table_ref, out_ref, *, slots, heads):
    block = QUERY_BLOCK
    offsets = tile_offsets()
    buckets = [bucket_of(offsets + shift * TILE) for shift in (-1, 0, 1)]
    for head in range(heads):
        tiles = []
        for marks in buckets:
            tile = jnp.full((TILE, TILE), table_ref[head, 0], WIDE)
            for bucket in range(1, BUCKETS):
                tile = jnp.where(marks == bucket, table_ref[head, bucket], tile)
            tiles.append(tile)
        for down in range((2 * slots - block) // TILE):
            for across in range(block // TILE):
                shift = down - (slots - block) // TILE - across
                if abs(shift) < 2:
                    tile = tiles[shift + 1]
                else:
                    far = table_ref[head, BUCKETS - 1 if shift > 0 else BUCKETS // 2 - 1]
                    tile = jnp.full((TILE, TILE), far, WIDE)
                out_ref[head, down * TILE : (down + 1) * TILE, across * TILE : (across + 1) * TILE] = tile


def bias_master(table, slots):
    heads = table.shape[0]
    shape = (heads, 2 * slots - QUERY_BLOCK, QUERY_BLOCK)
    return pl.pallas_call(
        functools.partial(bias_kernel, slots=slots, heads=heads),
        out_shape=jax.ShapeDtypeStruct(shape, WIDE),
        in_specs=[whole(pltpu.SMEM)],
        out_specs=whole(),
        compiler_params=pltpu.CompilerParams(vmem_limit_bytes=VMEM_LIMIT),
        cost_estimate=lasting(2),
        name="bias_master",
    )(table)


def whole(memory=pltpu.VMEM):
    return pl.BlockSpec(memory_space=memory)


def attend_forward(meta, rows_in, bias, slots, heads):
    width, block = heads * DK, QUERY_BLOCK
    return pl.pallas_call(
        functools.partial(forward_kernel, slots=slots, heads=heads),
        out_shape=(
            jax.ShapeDtypeStruct((slots, width), LOW),
            jax.ShapeDtypeStruct((8, slots), WIDE),
            jax.ShapeDtypeStruct((8, 128), WIDE),
        ),
        in_specs=[whole(pltpu.SMEM), whole(), whole()],
        out_specs=(whole(), whole(), whole()),
        scratch_shapes=[
            pltpu.VMEM((width, slots), WIDE),
            pltpu.VMEM((slots, block), jnp.int32),
        ],
        compiler_params=pltpu.CompilerParams(vmem_limit_bytes=VMEM_LIMIT),
        cost_estimate=lasting(10),
        name="attend_forward",
    )(meta, rows_in, bias)


def attend_backward(meta, rows_in, grad_in, log_total, bias, slots, heads):
    width, block = heads * DK, QUERY_BLOCK
    return pl.pallas_call(
        functools.partial(backward_kernel, slots=slots, heads=heads),
        out_shape=(
            jax.ShapeDtypeStruct((slots, 3 * width), LOW),
            jax.ShapeDtypeStruct((8, 128), WIDE),
        ),
        in_specs=[whole(pltpu.SMEM), whole(), whole(), whole(), whole()],
        out_specs=(whole(), whole()),
        scratch_shapes=[
            pltpu.VMEM((width, slots), WIDE),
            pltpu.VMEM((slots, block), jnp.int32),
            pltpu.VMEM((2 * slots - block, block), WIDE),
            pltpu.VMEM((slots, 2 * DK), WIDE),
        ],
        compiler_params=pltpu.CompilerParams(vmem_limit_bytes=VMEM_LIMIT),
        cost_estimate=lasting(15),
        name="attend_backward",
    )(meta, rows_in, grad_in, log_total, bias)


def gelu_with_slope(value):
    scale = math.sqrt(2.0 / math.pi)
    square = value * value
    bend = jnp.tanh(scale * (value + 0.044715 * value * square))
    active = 0.5 * value * (1.0 + bend)
    slope = 0.5 * (1.0 + bend) + 0.5 * value * (1.0 - bend * bend) * (scale * (1.0 + 3 * 0.044715 * square))
    return active, slope


def ffn_kernel(place_ref, rows_ref, grad_ref, *refs, count, units, tile):
    gates, ups, downs = (refs[n * count : (n + 1) * count] for n in range(3))
    product_ref, both_ref, terms_ref, pair_ref, down_ref = refs[3 * count :]
    depth = gates[0].shape[0]
    for n in range(count):
        span = pl.ds(pl.multiple_of((place_ref[0] ^ n) * depth, depth), depth)
        pair_ref[span, :units] = gates[n][...]
        pair_ref[span, units:] = ups[n][...]
        down_ref[span, :] = downs[n][...]

    def step(index, carry):
        rows = pl.ds(pl.multiple_of(index * tile, tile), tile)
        pre = contract(rows_ref[rows, :], pair_ref[...], 1, 0)
        grad_product = contract(grad_ref[rows, :], down_ref[...], 1, 0)
        upward = pre[:, units:]
        active, slope = gelu_with_slope(pre[:, :units])
        product_ref[rows, :] = (active * upward).astype(LOW)
        both_ref[rows, :units] = (grad_product * upward * slope).astype(LOW)
        both_ref[rows, units:] = (grad_product * active).astype(LOW)
        terms_ref[rows, :] = contract(both_ref[rows, :], pair_ref[...], 1, 1).astype(LOW)
        return carry

    lax.fori_loop(0, rows_ref.shape[0] // tile, step, 0)


def ffn_both_ways(place, rows_in, grad_in, gates, ups, downs):
    slots, model = rows_in.shape
    units = downs[0].shape[1]
    return pl.pallas_call(
        functools.partial(ffn_kernel, count=len(downs), units=units, tile=384),
        out_shape=(
            jax.ShapeDtypeStruct((slots, units), LOW),
            jax.ShapeDtypeStruct((slots, 2 * units), LOW),
            jax.ShapeDtypeStruct((slots, model), LOW),
        ),
        in_specs=[whole(pltpu.SMEM)] + [whole()] * (2 + 3 * len(downs)),
        out_specs=(whole(), whole(), whole()),
        scratch_shapes=[pltpu.VMEM((model, 2 * units), LOW), pltpu.VMEM((model, units), LOW)],
        compiler_params=pltpu.CompilerParams(vmem_limit_bytes=VMEM_LIMIT),
        cost_estimate=lasting(19),
        name="ffn_both_ways",
    )(place, rows_in, grad_in, *gates, *ups, *downs)


def ffn_out_kernel(place_ref, product_ref, *refs):
    pieces, terms_ref = refs[:-1], refs[-1]
    depth = pieces[0].shape[0]
    for n, piece in enumerate(pieces):
        span = pl.ds(pl.multiple_of((place_ref[0] ^ n) * depth, depth), depth)
        terms_ref[:, span] = contract(product_ref[...], piece[...], 1, 1).astype(LOW)


def ffn_out(place, product, pieces):
    slots, units = product.shape
    model = pieces[0].shape[0] * len(pieces)
    return pl.pallas_call(
        ffn_out_kernel,
        out_shape=jax.ShapeDtypeStruct((slots, model), LOW),
        in_specs=[whole(pltpu.SMEM)] + [whole()] * (1 + len(pieces)),
        out_specs=whole(),
        compiler_params=pltpu.CompilerParams(vmem_limit_bytes=VMEM_LIMIT),
        cost_estimate=lasting(5),
        name="ffn_out",
    )(place, product, *pieces)


def pack_kernel(gain_ref, *refs, count, scaled):
    parts, out_ref = refs[:-1], refs[-1]
    rows, width = parts[0].shape[0], parts[0].shape[1] // count
    for n, (part, scale) in enumerate(zip(parts, scaled, strict=True)):
        for block in range(count):
            piece = part[:, block * width : (block + 1) * width]
            if scale:
                piece = (piece.astype(WIDE) * gain_ref[...]).astype(LOW)
            out_ref[block * rows : (block + 1) * rows, n * width : (n + 1) * width] = piece


def pack(gain, parts, scaled, count):
    rows, columns = parts[0].shape
    return pl.pallas_call(
        functools.partial(pack_kernel, count=count, scaled=scaled),
        out_shape=jax.ShapeDtypeStruct((count * rows, len(parts) * columns // count), LOW),
        in_specs=[whole()] * (1 + len(parts)),
        out_specs=whole(),
        compiler_params=pltpu.CompilerParams(vmem_limit_bytes=VMEM_LIMIT),
        cost_estimate=lasting(2),
        name="pack",
    )(gain, *parts)


def shards(
    tokens,
    out_grad,
    lengths,
    w_query,
    w_key,
    w_value,
    w_out,
    w_gate,
    w_up,
    w_down,
    gain_attn,
    gain_ffn,
    bias_table,
    clip_limit,
):
    groups, count, cores = (lax.axis_size(name) for name in ("fsdp", "ctx", "tp"))
    assert cores == 2
    group, here, core = (lax.axis_index(name) for name in ("fsdp", "ctx", "tp"))
    half = tokens.shape[1] // cores
    slots = tokens.shape[1] * count
    heads = bias_table.shape[0] // count
    head_width = heads * DK
    unit_width = w_gate.shape[1] // count
    weight_rows = w_query.shape[0]

    def flip(value, mask):
        return lax.ppermute(value, "fsdp", [(i, i ^ mask) for i in range(groups)])

    def swap(value):
        return lax.ppermute(value, "tp", [(0, 1), (1, 0)])

    def spread(parts, gain, scaled):
        if parts[0].shape[1] // count % 128 == 0:
            packed = pack(gain, parts, scaled, count)
        else:
            parts = [(p.astype(WIDE) * gain).astype(LOW) if s else p for p, s in zip(parts, scaled, strict=True)]
            width = parts[0].shape[1] // count
            packed = jnp.concatenate(
                [
                    jnp.concatenate([p[:, n * width : (n + 1) * width] for p in parts], axis=1)
                    for n in range(count)
                ],
                axis=0,
            )
        return lax.all_to_all(packed, "ctx", 0, 0, tiled=True)

    def return_rows(block):
        return lax.all_to_all(block, "ctx", 0, 0, tiled=True)

    def collect(rows, width):
        blocks = [rows[n * weight_rows : (n + 1) * weight_rows] for n in range(count)]
        return [
            jnp.concatenate([b[:, at : at + width] for b in blocks], axis=1).astype(WIDE)
            for at in range(0, rows.shape[1], width)
        ]

    def pieces_of(block):
        return [block] + [flip(block, n) for n in range(1, groups)]

    def assemble(pieces):
        rows = pieces[0].shape[0]
        result = jnp.zeros((groups * rows, pieces[0].shape[1]), LOW)
        for n, piece in enumerate(pieces):
            mask, start, part = piece if isinstance(piece, tuple) else (n, 0, piece)
            result = lax.dynamic_update_slice_in_dim(result, part, (group ^ mask) * rows + start, 0)
        return result

    def gather_quickly(block):
        if groups != 4:
            pieces = pieces_of(block)
            return assemble(pieces), pieces[-1]
        middle = block.shape[0] // 2
        first, second = flip(block, 1), flip(block, 2)
        low, high = flip(first[:middle], 2), flip(second[middle:], 1)
        return assemble([block, first, second, (3, 0, low), (3, middle, high)]), first, second

    def blocks_of(terms):
        rows = terms.shape[0] // groups
        return [lax.dynamic_slice_in_dim(terms, (group ^ n) * rows, rows, 0) for n in range(groups)]

    def flip_blocks(blocks):
        return [block if n == 0 else flip(block, n) for n, block in enumerate(blocks)]

    def sum_of(blocks):
        return sum(block.astype(WIDE) for block in blocks).astype(LOW)

    def reduce_weights(terms):
        return sum_of(flip_blocks(blocks_of(terms)))

    def after(value, *earlier):
        return lax.optimization_barrier((value, *earlier))[0]

    def together(*values):
        return lax.optimization_barrier(values)

    def gather_rows(piece):
        return lax.all_gather(piece, ("ctx", "tp"), axis=0, tiled=True)

    def reduce_rows(terms):
        return lax.psum_scatter(terms.astype(LOW), ("ctx", "tp"), scatter_dimension=0, tiled=True).astype(WIDE)

    def feed_forward(place, rows_in, grad_in, gate, up, down):
        if unit_width % 128 == 0:
            return ffn_both_ways(place, rows_in, grad_in, gate, up, down)
        gate, up, down = (assemble(pieces) for pieces in (gate, up, down))
        upward = contract(rows_in, up, 1, 0)
        active, slope = gelu_with_slope(contract(rows_in, gate, 1, 0))
        grad_product = contract(grad_in, down, 1, 0)
        product = (active * upward).astype(LOW)
        both = jnp.concatenate([grad_product * upward * slope, grad_product * active], axis=1).astype(LOW)
        terms = contract(both[:, :unit_width], gate, 1, 1) + contract(both[:, unit_width:], up, 1, 1)
        return product, both, terms.astype(LOW)

    def feed_forward_out(place, product, down):
        if unit_width % 128 == 0:
            return ffn_out(place, product, down)
        return contract(product, assemble(down), 1, 1).astype(LOW)

    def both_cores(piece):
        other = swap(piece)
        return jnp.where(
            core == 0, jnp.concatenate([piece, other], axis=0), jnp.concatenate([other, piece], axis=0)
        )

    def own_rows(value):
        return lax.dynamic_slice_in_dim(value[0], core * half, half, 0)

    def inverse_norm(value):
        return lax.rsqrt(jnp.mean(value * value, axis=-1, keepdims=True) + EPSILON)

    def norm_back(value, inverse, grad):
        along = jnp.mean(grad * value, axis=-1, keepdims=True)
        return inverse * grad - value * (inverse * inverse * inverse * along)

    ends = (lengths[0, 0], lengths[0, 0] + lengths[0, 1])
    meta = jnp.stack(ends).astype(jnp.int32)
    attn_gain = gain_attn.astype(WIDE)[:, None]
    ffn_gain = gain_ffn.astype(WIDE)[:, None]

    inputs = own_rows(tokens).astype(WIDE)
    inverse_one = inverse_norm(inputs)
    row_place = (here * cores + core) * half + jnp.arange(half, dtype=jnp.int32)
    row_valid = (row_place < ends[1])[:, None]
    grad_out = jnp.where(row_valid, own_rows(out_grad).astype(WIDE), 0.0)
    my_table = lax.dynamic_slice_in_dim(bias_table, here * heads, heads, 0).astype(WIDE)

    bias = bias_master(my_table, slots)
    attn_mine = after(
        spread([w_query, w_key, w_value, w_out], attn_gain, (True, True, True, False)), bias
    )
    normed_rows = gather_rows(after((inputs * inverse_one).astype(LOW), attn_mine))
    all_columns, *arrived = gather_quickly(attn_mine)
    attn_columns, out_columns = all_columns[:, : 3 * head_width], all_columns[:, 3 * head_width :]
    gate_mine = spread([after(w_gate, attn_mine)], ffn_gain, (True,))
    normed = after(normed_rows, all_columns, gate_mine)
    grad_rows = gather_rows(after(grad_out.astype(LOW), *arrived))

    projected = contract(normed, attn_columns, 1, 0).astype(LOW)
    gate_pieces = pieces_of(after(gate_mine, all_columns))
    mixed, log_total, peaks = attend_forward(meta, projected, bias, slots, heads)
    branch_terms = contract(mixed, out_columns, 1, 1).astype(LOW)
    up_mine = spread([after(w_up, normed)], ffn_gain, (True,))
    branch_terms = after(branch_terms, grad_rows, up_mine, *gate_pieces)
    down_mine = spread([after(w_down, up_mine)], ffn_gain, (False,))
    up_pieces = pieces_of(after(up_mine, *gate_pieces))
    branch = after(reduce_rows(branch_terms), down_mine, *up_pieces)
    down_pieces = pieces_of(after(down_mine, *up_pieces))
    hidden = inputs + branch
    inverse_two = inverse_norm(hidden)
    normed_ffn = gather_rows((hidden * inverse_two).astype(LOW))

    place = group.astype(jnp.int32)[None]
    product, grad_both, ffn_terms = feed_forward(place, normed_ffn, grad_rows, gate_pieces, up_pieces, down_pieces)
    grad_normed_ffn = reduce_rows(ffn_terms)
    out_terms = feed_forward_out(place, after(product, ffn_terms), down_pieces)
    gate_terms = contract(after(normed_ffn, ffn_terms), grad_both[:, :unit_width], 0, 0).astype(LOW)
    up_terms = contract(after(normed_ffn, ffn_terms), grad_both[:, unit_width:], 0, 0).astype(LOW)
    down_terms = contract(after(grad_rows, ffn_terms), product, 0, 0).astype(LOW)
    first_sum = reduce_weights(gate_terms)
    grad_normed_ffn = after(grad_normed_ffn, first_sum, up_terms, down_terms, out_terms)
    grad_hidden = grad_out + norm_back(hidden, inverse_two, grad_normed_ffn)
    branch_low = grad_hidden.astype(LOW)
    cut = unit_width * 3 // 5
    second_blocks = [
        jnp.concatenate(pair, axis=1)
        for pair in zip(blocks_of(up_terms), blocks_of(down_terms[:, :cut]), strict=True)
    ]
    second_sum = sum_of(flip_blocks(second_blocks))
    gathered = gather_rows(branch_low)
    branch_rows, second_sum = together(gathered, second_sum)
    ffn_out_sum = reduce_rows(after(out_terms, gathered))

    grad_mixed = contract(branch_rows, out_columns, 1, 0).astype(LOW)
    units = jnp.concatenate([first_sum, second_sum], axis=1)
    units = after(units, grad_mixed)
    grad_projected, table_terms = attend_backward(
        meta, projected, grad_mixed, log_total, bias, slots, heads
    )
    units_back = return_rows(units)
    third_blocks = blocks_of(after(down_terms[:, cut:], second_sum))
    out_blocks = blocks_of(contract(branch_rows, after(mixed, grad_mixed), 0, 0).astype(LOW))
    third_sum = sum_of(
        flip_blocks([jnp.concatenate(pair, axis=1) for pair in zip(out_blocks, third_blocks, strict=True)])
    )
    grad_projected, third_sum = together(grad_projected, third_sum)
    attn_terms = contract(normed, grad_projected, 0, 0).astype(LOW)
    attn_sum = reduce_weights(attn_terms)
    grad_normed = reduce_rows(contract(after(grad_projected, attn_terms), attn_columns, 1, 1))
    attn_sum, units_back = together(attn_sum, units_back)
    attn_back = return_rows(jnp.concatenate([attn_sum, third_sum], axis=1))
    grad_query_w, grad_key_w, grad_value_w, grad_out_w = collect(attn_back[:, : 4 * head_width], head_width)
    grad_gate_w, grad_up_w = collect(units_back[:, : 2 * unit_width], unit_width)
    (grad_down,) = collect(
        jnp.concatenate([units_back[:, 2 * unit_width :], attn_back[:, 4 * head_width :]], axis=1), unit_width
    )
    mixed_out = both_cores((hidden + ffn_out_sum).astype(LOW))[None]
    grad_tokens = both_cores((grad_hidden + norm_back(inputs, inverse_one, grad_normed)).astype(LOW))[None]

    def gain_terms(weights, grads):
        return sum(jnp.sum(w.astype(WIDE) * g, axis=1) for w, g in zip(weights, grads, strict=True))

    gain_grads = jnp.stack(
        [
            gain_terms((w_query, w_key, w_value), (grad_query_w, grad_key_w, grad_value_w)),
            gain_terms((w_gate, w_up), (grad_gate_w, grad_up_w)),
        ]
    )
    gain_grads = gain_grads + swap(gain_grads)

    table_terms = after(table_terms, attn_sum)
    small = jnp.concatenate([table_terms[:heads, :BUCKETS], peaks[:heads, :1]], axis=1)
    blank = jnp.concatenate([jnp.zeros((1, BUCKETS), WIDE), jnp.full((1, 1), NEGATIVE, WIDE)], axis=1)
    is_sum = jnp.arange(BUCKETS + 1)[None, :] < BUCKETS
    small = jnp.where(
        (jnp.arange(count * heads) // heads == here)[:, None],
        jnp.tile(small, (count, 1)),
        blank,
    )

    def merge(first, second):
        return jnp.where(is_sum, first + second, jnp.maximum(first, second))

    mask = 1
    while mask < groups:
        small = merge(small, flip(small, mask))
        mask *= 2
    mask = 1
    while mask < count:
        small = merge(small, lax.ppermute(small, "ctx", [(i, i ^ mask) for i in range(count)]))
        mask *= 2
    grad_table, head_peaks = small[:, :BUCKETS], small[:, BUCKETS]
    factor = jnp.sqrt(clip_limit / jnp.maximum(head_peaks, clip_limit))
    factor_row = jnp.repeat(factor, DK)[None, :]

    def clipped(weight):
        return (weight.astype(WIDE) * factor_row).astype(LOW)

    return (
        mixed_out,
        grad_tokens,
        grad_query_w * attn_gain,
        grad_key_w * attn_gain,
        grad_value_w * attn_gain,
        grad_out_w,
        grad_gate_w * ffn_gain,
        grad_up_w * ffn_gain,
        grad_down,
        gain_grads[0],
        gain_grads[1],
        grad_table,
        head_peaks,
        clipped(w_query),
        clipped(w_key),
    )


def solution(mesh):
    rows, weight, gain = P("fsdp", "ctx", None), P(("fsdp", "ctx"), "tp"), P(("fsdp", "ctx"))
    return jax.shard_map(
        shards,
        mesh=mesh,
        in_specs=(rows, rows, P("fsdp", None)) + (weight,) * 7 + (gain, gain, P("tp", None), P("tp")),
        out_specs=(rows, rows) + (weight,) * 7 + (gain, gain, P("tp", None), P("tp"), weight, weight),
        check_vma=False,
    )
```
